512 devices in a mesh: fsdp: 32 (over y, x), ctx: 8 (over z), tp: 2 (over core).
Axes of the slice: x: 4, y: 8, z: 8, core: 2. Of those that a mesh axis runs over, the one named last changes fastest.
Arguments:
- tokens: bfloat16 [1, 4096, 8192], P(None, 'ctx', ('fsdp', 'tp')), may hold values from -6 to 6
- w_in: bfloat16 [8192, 3, 8192], P('ctx', None, ('fsdp', 'tp')), may hold values from -0.0625 to 0.0625
- short_taps: float32 [7, 3, 8192], P(None, None, ('fsdp', 'tp')), may hold values from -2 to 2
- mr_taps: float32 [128, 8192], P(None, ('fsdp', 'tp')), may hold values from -1 to 1
- skip: float32 [8192], P(('fsdp', 'tp')), may hold values from 0.5 to 1.5
- genome_ids: int32 [1, 4096], replicated, may hold values from 0 to 3, never falling along the last dimension, each value on 1 to 2048 neighbouring positions
Outputs:
- gated: bfloat16 [1, 4096, 8192], P(None, 'ctx', ('fsdp', 'tp'))
The draws below stay inside these ranges and needn't reach their ends.
Inputs may be any that keep to these rules, and one draw needn't show every extreme that they name: `genome_ids`: ids never fall along a sequence; each genome holds 1 to 2048 positions, and one holds exactly 2048.
All inputs are finite; a program needn't handle non-finite values.
Results may differ from the reference program's by a relative error of at most 0.007.
Values may be sent and summed in bfloat16 or wider, within the bound.
No kernel may reach another device: no remote copies, remote signals or barrier semaphores. Data moves between devices by JAX's collectives and lax.ppermute only.
A program may use at most 64 MiB of HBM per device.

```python
import math
import jax
import jax.numpy as jnp
import numpy as np
from jax import lax

D = 8192
CH = 8192
SHORT = 7
TAPS = 128
SEQS = 1
GENOMES = 4
LENGTH = 4096
GMOST = 2048


def levels(own_key, dims, shards, smallest, top_value):
    loudness = 1.0
    for position, blocks in shards:
        steps = jax.random.uniform(jax.random.fold_in(jax.random.fold_in(own_key, 6), position), (blocks,), jnp.float32, smallest / len(shards), top_value / len(shards))
        loudness = loudness * jnp.repeat(jnp.exp(steps), dims[position] // blocks).reshape((-1,) + (1,) * (len(dims) - 1 - position))
    return loudness


def split_up(amount, total, bound, lean):
    weights = [(1 << 20) // math.isqrt(grade ** lean) + 1 for grade in range(2, amount + 1)]
    rest, given = total - bound - (amount - 1), [1] * (amount - 1)
    while rest > 0:
        free = [i for i in range(amount - 1) if given[i] < bound]
        pool, budget = sum([weights[i] for i in free]), rest
        for i in free:
            more = min(bound - given[i], max(1, budget * weights[i] // pool), rest)
            given[i] = given[i] + more
            rest = rest - more
    return np.array([bound] + given)


def ragged(stream_key, number_of, total, most, slope):
    if number_of == 2:
        one = jax.random.randint(stream_key, (), max(1, total - most), min(most, total - 1) + 1)
        return jnp.stack([one, total - one])
    lengths = jnp.asarray(split_up(number_of, total, most, slope), jnp.int32)
    pairs = (number_of - 1) // 2
    giver, taker = lengths[1:1 + 2 * pairs:2], lengths[2:2 + 2 * pairs:2]
    room = jnp.minimum(giver - 1, most - taker)
    moved = jax.random.randint(jax.random.fold_in(stream_key, 1), (pairs,), 0, 1 << 20) % (room + 1)
    lengths = lengths.at[1:1 + 2 * pairs:2].set(giver - moved).at[2:2 + 2 * pairs:2].set(taker + moved)
    return lengths[jax.random.permutation(jax.random.fold_in(stream_key, 2), number_of)]


def centred(key, dims, scale, most, pieces=(), held_as=jnp.bfloat16):
    values = scale * jax.random.normal(key, dims, jnp.float32)
    if pieces:
        values = values * levels(key, dims, pieces, -0.22, 0.18)
    return jnp.clip(values, -most, most).astype(held_as)


def setup_inputs(seed: int = 0) -> dict:
    keys = jax.random.split(jax.random.key(seed), 7)
    tokens = centred(keys[0], (SEQS, LENGTH, D), 1.0, 6.0, ((1, 8), (2, 64)))
    w_in = centred(keys[1], (D, 3, CH), D ** -0.5, 0.0625, ((0, 8), (2, 64)))
    short_taps = centred(keys[2], (SHORT, 3, CH), 0.4, 2.0, ((2, 64),), jnp.float32)
    mr_taps = centred(keys[3], (TAPS, CH), 32 ** -0.5, 1.0, ((1, 64),), jnp.float32)
    skip = jnp.clip(0.5 + 1.0 * jax.random.uniform(keys[4], (CH,), jnp.float32) ** levels(keys[4], (CH,), ((0, 64),), -0.2, 0.2), 0.5, 1.5)
    genome_ids = jax.vmap(lambda own: jnp.searchsorted(jnp.cumsum(ragged(own, GENOMES, LENGTH, GMOST, 2)), jnp.arange(LENGTH), side="right"))(jax.random.split(keys[5], SEQS)).reshape((SEQS, LENGTH)).astype(jnp.int32)
    return dict(tokens=tokens, w_in=w_in, short_taps=short_taps, mr_taps=mr_taps, skip=skip, genome_ids=genome_ids)


def causal_mix(padded, segment_pad, taps, count):
    reach = taps.shape[0] - 1
    target = segment_pad[:, reach:reach + count]

    def add_lag(offset, total):
        piece = lax.dynamic_slice_in_dim(padded, reach - offset, count, 1).astype(jnp.float32)
        source = lax.dynamic_slice_in_dim(segment_pad, reach - offset, count, 1)
        same = (source == target).astype(jnp.float32)[..., None]
        weight = lax.dynamic_index_in_dim(taps, offset, 0, keepdims=False)
        return total + weight * piece * same

    start = jnp.zeros(padded.shape[:1] + (count,) + padded.shape[2:], jnp.float32)
    return lax.fori_loop(0, reach + 1, add_lag, start)


def reference(tokens, w_in, short_taps, mr_taps, skip, genome_ids):
    channels = w_in.shape[2]
    length = tokens.shape[1]
    panel_all = w_in.reshape(w_in.shape[0], -1)
    raw = lax.map(lambda token_rows: jnp.dot(token_rows, panel_all, preferred_element_type=jnp.float32).astype(jnp.bfloat16), tokens)
    short_reach = short_taps.shape[0] - 1
    long_reach = mr_taps.shape[0] - 1
    raw_pad = jnp.pad(raw, ((0, 0), (short_reach, 0), (0, 0)))
    segment_short = jnp.pad(genome_ids, ((0, 0), (short_reach, 0)), constant_values=-1)
    featured = causal_mix(raw_pad, segment_short, short_taps.reshape(short_taps.shape[0], -1), length)
    queries = featured[..., :channels]
    keys_in = featured[..., channels:2 * channels]
    values_in = featured[..., 2 * channels:]
    mixed = (keys_in * values_in).astype(jnp.bfloat16)
    mixed_pad = jnp.pad(mixed, ((0, 0), (long_reach, 0), (0, 0)))
    segment_long = jnp.pad(genome_ids, ((0, 0), (long_reach, 0)), constant_values=-1)
    filtered = causal_mix(mixed_pad, segment_long, mr_taps, length)
    return (queries * (filtered + skip * mixed.astype(jnp.float32))).astype(jnp.bfloat16)
```

```python
import functools

import jax
import jax.numpy as jnp
from jax import lax
from jax.experimental import pallas as pl
from jax.experimental.pallas import tpu as pltpu
from jax.sharding import PartitionSpec as P

HALO = 16
GROUP = 64
BF16, F32 = jnp.bfloat16, jnp.float32
VMEM = pl.BlockSpec(memory_space=pltpu.VMEM)
SMEM = pl.BlockSpec(memory_space=pltpu.SMEM)
ANY = pl.BlockSpec(memory_space=pl.ANY)
MIB = 1 << 20


def call(kernel, out_shape, in_specs, out_specs, scratch=(), flops=0, nbytes=0, vmem=8):
    return pl.pallas_call(
        kernel,
        out_shape=out_shape,
        in_specs=in_specs,
        out_specs=out_specs,
        scratch_shapes=list(scratch),
        compiler_params=pltpu.CompilerParams(vmem_limit_bytes=vmem * MIB),
        cost_estimate=pl.CostEstimate(flops=flops, bytes_accessed=nbytes, transcendentals=0),
    )


def product(token_block, weights):
    left = jnp.concatenate([token_block[j] for j in range(token_block.shape[0])], 1)
    right = jnp.concatenate([weights[g] for g in range(3)], 1)
    return jnp.dot(left, right, preferred_element_type=F32)


def first_sums(count, done, offsets, place, ids, ends, *refs):
    blocks, refs = refs[:count], refs[count:]
    theirs, mine, refs = refs[:done], refs[done : 2 * done], refs[2 * done :]
    theirs_ref, mine_ref, last_ref, held, sem = refs
    y, z, step = place[0], place[1], place[2]
    copies = []
    for k, offset in enumerate(offsets):
        slot = lax.rem(y + offset + count, count)
        copies.append(pltpu.make_async_copy(blocks[k], held.at[slot], sem.at[k]))
    for copy in copies:
        copy.start()
    for copy in copies:
        copy.wait()
    for weights, out in ((theirs, theirs_ref), (mine, mine_ref)):
        for s in range(done):
            slot = lax.rem(z + s * step + s * count, count)
            term = product(held[slot], weights[s])
            if s == 0:
                out[...] = term
            else:
                out[...] += term
    last_ref[...] = held[lax.rem(z + done * step + done * count, count)]


def last_theirs(block, weights, total, out):
    out[...] = (total[...] + product(block, weights)).astype(out.dtype)


def feature(block, weights, total, received, ids, taps, mixed_ref, queries_ref, raw):
    rows = mixed_ref.shape[0]
    summed = total[...] + product(block, weights) + received[...].astype(F32)
    raw[...] = summed.astype(BF16).astype(F32)
    reach = taps.shape[0] - 1
    step = 64

    def part(i, _):
        base = pl.multiple_of(i * step, step)
        near = ids[pl.ds(base + ids.shape[0] - rows - HALO, step + HALO), :]
        held = [raw[pl.ds(base, step + HALO), 128 * g : 128 * g + 128] for g in range(3)]
        sums = [jnp.zeros((step, 128), F32) for _ in range(3)]
        for lag in range(reach + 1):
            spot = slice(HALO - lag, HALO - lag + step)
            same = near[spot] == near[HALO:]
            for g in range(3):
                piece = held[g][spot]
                weight = taps[lag : lag + 1, 128 * g : 128 * g + 128]
                sums[g] = sums[g] + jnp.where(same, piece * weight, 0.0)
        queries_ref[pl.ds(base, step), :] = sums[0]
        mixed_ref[pl.ds(base, step), :] = (sums[1] * sums[2]).astype(BF16)
        return 0

    lax.fori_loop(0, rows // step, part, 0)


def long_filter(first, last, reach, ends, mixed, ids, queries, taps, skip, out, source, window):
    def group(i, _):
        base = pl.multiple_of(first + i * GROUP, GROUP)
        here = ids[pl.ds(base + reach, GROUP), :]

        def genome(g, total):
            for k in range((reach + GROUP) // GROUP):
                spot = pl.ds(base + k * GROUP, GROUP)
                window[k * GROUP : k * GROUP + GROUP, :] = jnp.where(
                    ids[spot, :] == g, source[spot, :], 0.0
                )

            sums = jnp.zeros((GROUP, 128), F32)
            for s in range(8):
                held = window[8 - s : GROUP + reach - s, :]
                for a in range(reach // 8):
                    weight = taps[8 * a + s : 8 * a + s + 1, :]
                    start = reach - 8 - 8 * a
                    sums = sums + held[start : start + GROUP] * weight
            return jnp.where(here == g, sums, total)

        low, high = ends[2 * (base // GROUP)], ends[2 * (base // GROUP) + 1]
        total = lax.fori_loop(low, high + 1, genome, jnp.zeros((GROUP, 128), F32))
        bias = skip[...] * source[pl.ds(base + reach, GROUP), :]
        gated = queries[pl.ds(base, GROUP), :] * (total + bias)
        out[pl.ds(base, GROUP), :] = gated.astype(out.dtype)
        return 0

    lax.fori_loop(0, (last - first) // GROUP, group, 0)


def filter_main(reach, ends, mixed, ids, queries, taps, skip, out, source, window):
    rows = mixed.shape[0]
    source[reach:, :] = mixed[...].astype(F32)
    long_filter(reach, rows, reach, ends, mixed, ids, queries, taps, skip, out, source, window)


def filter_head(reach, ends, earlier, mixed, ids, queries, taps, skip, given, out, source, window):
    source[:reach, :] = earlier[...].astype(F32)
    source[reach:, :] = mixed[:reach, :].astype(F32)
    out[reach:, :] = given[reach:, :]
    long_filter(0, reach, reach, ends, mixed, ids, queries, taps, skip, out, source, window)


def body(tokens, w_in, short_taps, mr_taps, skip, genome_ids):
    length, width = tokens.shape[1], tokens.shape[2]
    ctx, tp = lax.axis_size("ctx"), lax.axis_size("tp")
    xs, ys = lax.axis_size("fsdp") // ctx, ctx
    reach = mr_taps.shape[0]
    f, z, c = lax.axis_index("fsdp"), lax.axis_index("ctx"), lax.axis_index("tp")
    x, y = f % xs, f // xs

    along_x = lambda d: [(j * xs + i, j * xs + (i + d) % xs) for j in range(ys) for i in range(xs)]
    along_y = lambda d: [(j * xs + i, (j + d) % ys * xs + i) for j in range(ys) for i in range(xs)]
    ring = [(k * tp + t, (k + 1 - 2 * t) % ctx * tp + t) for k in range(ctx) for t in range(tp)]
    swap = [(0, 1), (1, 0)]

    planes = jnp.transpose(w_in, (1, 0, 2)).reshape(3, xs, tp, width, width)
    mine = lax.dynamic_index_in_dim(planes, c, 2, False).reshape(3, xs * width, width)
    theirs = lax.dynamic_index_in_dim(planes, 1 - c, 2, False).reshape(3, xs * width, width)
    mine, theirs = [mine], [lax.ppermute(theirs, "tp", swap)]
    for _ in range(ctx - 1):
        theirs.append(lax.ppermute(theirs[-1], ("ctx", "tp"), ring))
        mine.append(lax.ppermute(mine[-1], ("ctx", "tp"), ring))

    own = tokens[0]
    before = lax.ppermute(own[length - HALO :], "ctx", [(k, (k + 1) % ctx) for k in range(ctx)])
    own = jnp.concatenate([before, own], 0)
    block = jnp.zeros((xs,) + own.shape, BF16)
    block = lax.dynamic_update_index_in_dim(block, own, x, 0)
    for d in range(1, xs):
        hop = d if d <= xs // 2 else d - xs
        piece = lax.ppermute(own, "fsdp", along_x(hop))
        block = lax.dynamic_update_index_in_dim(block, piece, (x - hop) % xs, 0)
    blocks, offsets = [block], [0]
    up = down = block
    for s in range(1, ys // 2 + 1):
        up = lax.ppermute(up, "fsdp", along_y(1))
        blocks.append(up)
        offsets.append(-s)
        if s <= (ys - 1) // 2:
            down = lax.ppermute(down, "fsdp", along_y(-1))
            blocks.append(down)
            offsets.append(s)

    start = z * length
    padded = jnp.pad(genome_ids[0], (reach, 0), constant_values=-1)
    seen = lax.dynamic_slice_in_dim(padded, start, length + reach, 0)
    ids = jnp.broadcast_to(seen[:, None], (length + reach, 128))
    ends = jnp.stack([seen[reach::GROUP], seen[reach + GROUP - 1 :: GROUP]], 1).reshape(-1)
    place = jnp.stack([y, z, 2 * c - 1]).astype(jnp.int32)

    rows, done = length + HALO, ctx - 1
    wide = jax.ShapeDtypeStruct((rows, 3 * width), F32)
    taken = jax.ShapeDtypeStruct((xs, rows, width), BF16)
    one = 2 * rows * xs * width * 3 * width
    sum_theirs, sum_mine, last = call(
        functools.partial(first_sums, ys, done, tuple(offsets)),
        (wide, wide, taken),
        [SMEM, ANY, ANY] + [ANY] * ys + [VMEM] * (2 * done),
        (VMEM, VMEM, VMEM),
        [pltpu.VMEM((ys, xs, rows, width), BF16), pltpu.SemaphoreType.DMA((ys,))],
        flops=2 * done * one,
        nbytes=12 << 20,
        vmem=16,
    )(place, ids, ends, *blocks, *theirs[:done], *mine[:done])
    give = call(
        last_theirs,
        jax.ShapeDtypeStruct((rows, 3 * width), BF16),
        [VMEM] * 3,
        VMEM,
        flops=one,
        nbytes=2 << 20,
    )(last, theirs[done], sum_theirs)
    received = lax.ppermute(give, "tp", swap)
    mixed, queries = call(
        feature,
        (jax.ShapeDtypeStruct((length, width), BF16), jax.ShapeDtypeStruct((length, width), F32)),
        [VMEM] * 6,
        (VMEM, VMEM),
        [pltpu.VMEM((rows, 3 * width), F32)],
        flops=one,
        nbytes=4 << 20,
    )(
        last,
        mine[done],
        sum_mine,
        received,
        ids,
        short_taps.reshape(short_taps.shape[0], -1),
    )
    earlier = lax.ppermute(mixed[length - reach :], "ctx", [(k, (k + 1) % ctx) for k in range(ctx)])
    bias = skip[None, :]
    outline = jax.ShapeDtypeStruct((length, width), BF16)
    part = call(
        functools.partial(filter_main, reach),
        outline,
        [SMEM] + [VMEM] * 5,
        VMEM,
        [pltpu.VMEM((reach + length, width), F32), pltpu.VMEM((reach + GROUP, width), F32)],
        flops=2 * (length - reach) * width * reach,
        nbytes=1 << 20,
    )(ends, mixed, ids, queries, mr_taps, bias)
    gated = call(
        functools.partial(filter_head, reach),
        outline,
        [SMEM] + [VMEM] * 7,
        VMEM,
        [pltpu.VMEM((2 * reach, width), F32), pltpu.VMEM((reach + GROUP, width), F32)],
        flops=2 * reach * width * reach,
        nbytes=1 << 20,
    )(ends, earlier, mixed, ids, queries, mr_taps, bias, part)
    return gated[None]


def solution(mesh):
    in_specs = (
        P(None, "ctx", ("fsdp", "tp")),
        P("ctx", None, ("fsdp", "tp")),
        P(None, None, ("fsdp", "tp")),
        P(None, ("fsdp", "tp")),
        P(("fsdp", "tp")),
        P(),
    )
    out_specs = P(None, "ctx", ("fsdp", "tp"))
    return jax.shard_map(body, mesh=mesh, in_specs=in_specs, out_specs=out_specs, check_vma=False)
```

```python
import functools

import jax
import jax.numpy as jnp
from jax import lax
from jax.experimental import pallas as pl
from jax.experimental.pallas import tpu as pltpu
from jax.sharding import PartitionSpec as P

PAD = 16
LEAD = 128 + PAD
HEAD = 192
STEP = 64
CHUNK = 2
GROUP = 64
BF16, F32 = jnp.bfloat16, jnp.float32
VMEM = pl.BlockSpec(memory_space=pltpu.VMEM)
SMEM = pl.BlockSpec(memory_space=pltpu.SMEM)
ANY = pl.BlockSpec(memory_space=pl.ANY)
HBM = pl.BlockSpec(memory_space=pltpu.HBM)
MIB = 1 << 20


def call(kernel, out_shape, in_specs, out_specs, scratch=(), flops=0, nbytes=0, vmem=8):
    return pl.pallas_call(
        kernel,
        out_shape=out_shape,
        in_specs=in_specs,
        out_specs=out_specs,
        scratch_shapes=list(scratch),
        compiler_params=pltpu.CompilerParams(vmem_limit_bytes=vmem * MIB),
        cost_estimate=pl.CostEstimate(flops=flops, bytes_accessed=nbytes, transcendentals=0),
    )


def wide(planes, groups=None):
    return jnp.concatenate([planes[j] for j in range(planes.shape[0])], 1)


def fetch(pairs, sem):
    copies = [pltpu.make_async_copy(src, dst, sem.at[k]) for k, (src, dst) in enumerate(pairs)]
    for copy in copies:
        copy.start()
    return copies


def product(blocks, weights, ready):
    total = None
    for s in range(0, blocks.shape[0], CHUNK):
        these = range(s, s + CHUNK)
        for t in these:
            ready(t)
        left = [blocks[t, j] for t in these for j in range(blocks.shape[1])]
        right = [wide(weights[t]) for t in these]
        term = jnp.dot(
            jnp.concatenate(left, 1), jnp.concatenate(right, 0), preferred_element_type=F32
        )
        total = term if total is None else total + term
    return total


def theirs_sum(count, tokens_from, weights_from, place, ids, ends, *refs):
    token_refs, weight_refs = refs[:count], refs[count : 2 * count]
    out, held_out, held, weights, sem, out_sem = refs[2 * count :]
    pairs, kept = [], []
    for k in range(count):
        slot = lax.rem(place[0] + tokens_from[k] + count, count)
        pairs.append((token_refs[k], held.at[slot]))
        kept.append((token_refs[k], held_out.at[slot]))
        slot = lax.rem(place[1] + weights_from[k] + count, count)
        pairs.append((weight_refs[k], weights.at[slot]))
    copies = fetch(pairs, sem)
    kept = fetch(kept, out_sem)
    for copy in copies:
        copy.wait()
    out[...] = product(held, weights, lambda t: None).astype(out.dtype)
    for copy in kept:
        copy.wait()


def mine_sum(held_in, weights_in, held, weights, sem):
    count, rows = held.shape[0], held.shape[2]
    first = held_in.shape[2] - rows
    pairs = []
    for t in range(count):
        pairs.append((held_in.at[t, :, first:, :], held.at[t]))
        pairs.append((weights_in.at[t], weights.at[t]))
    copies = fetch(pairs, sem)

    def ready(t):
        copies[2 * t].wait()
        copies[2 * t + 1].wait()

    return product(held, weights, ready)


def rim_sum(held_in, weights_in, received, out, held, weights, sem):
    first = received.shape[0] - out.shape[0]
    total = mine_sum(held_in, weights_in, held, weights, sem)
    out[...] = (total + received[first:, :].astype(F32)).astype(BF16)


def features(first, last, shift, raw, ids, taps, mixed, queries):
    reach = taps.shape[0] - 1
    for base in range(first, last, STEP):
        step = min(STEP, last - base)
        near = ids[base + LEAD - PAD : base + LEAD + step, :]
        begin = base + shift - PAD
        sums = [jnp.zeros((step, 128), F32) for _ in range(3)]
        for g in range(3):
            if g == 0 and base < 0:
                continue
            held = raw[begin : begin + PAD + step, 128 * g : 128 * g + 128]
            for lag in range(reach + 1):
                spot = slice(PAD - lag, PAD - lag + step)
                weight = taps[lag : lag + 1, 128 * g : 128 * g + 128]
                same = near[spot] == near[PAD:]
                sums[g] = sums[g] + jnp.where(same, held[spot] * weight, 0.0)
        if base >= 0:
            queries[base : base + step, :] = sums[0]
        mixed[base + shift : base + shift + step, :] = (sums[1] * sums[2]).astype(BF16).astype(F32)


def long_filter(first, last, shift, ends, ids, mixed, queries, taps, skip, out, window):
    reach = taps.shape[0]

    def group(i, _):
        base = pl.multiple_of(first + i * GROUP, GROUP)
        here = ids[pl.ds(base + LEAD, GROUP), :]

        def genome(g, total):
            for k in range((reach + GROUP) // GROUP):
                spot = pl.ds(base + k * GROUP + LEAD - reach, GROUP)
                source = pl.ds(pl.multiple_of(base + k * GROUP + shift - reach, PAD), GROUP)
                window[k * GROUP : k * GROUP + GROUP, :] = jnp.where(
                    ids[spot, :] == g, mixed[source, :], 0.0
                )
            sums = jnp.zeros((GROUP, 128), F32)
            for s in range(8):
                held = window[8 - s : GROUP + reach - s, :]
                for a in range(reach // 8):
                    weight = taps[8 * a + s : 8 * a + s + 1, :]
                    start = reach - 8 - 8 * a
                    sums = sums + held[start : start + GROUP] * weight
            return jnp.where(here == g, sums, total)

        low, high = ends[2 * (base // GROUP)], ends[2 * (base // GROUP) + 1]
        total = lax.fori_loop(low, high + 1, genome, jnp.zeros((GROUP, 128), F32))
        bias = skip[...] * mixed[pl.ds(pl.multiple_of(base + shift, PAD), GROUP), :]
        gated = queries[pl.ds(base, GROUP), :] * (total + bias)
        out[pl.ds(base, GROUP), :] = gated.astype(out.dtype)
        return 0

    lax.fori_loop(0, (last - first) // GROUP, group, 0)


def main_part(
    ends, held_in, weights_in, received, ids, short, taps, skip, out, top,
    raw, mixed, queries, window, held, weights, sem,
):
    rows = held.shape[2]
    summed = mine_sum(held_in, weights_in, held, weights, sem) + received[...].astype(F32)
    rounded = summed.astype(BF16)
    top[...] = rounded[: top.shape[0]]
    raw[...] = rounded.astype(F32)
    features(PAD, rows, 0, raw, ids, short, mixed, queries)
    long_filter(HEAD, rows, 0, ends, ids, mixed, queries, taps, skip, out, window)


def head_part(ends, before, top, ids, short, taps, skip, given, out, raw, mixed, queries, window):
    rim = before.shape[0]
    raw[:rim, :] = before[...].astype(F32)
    raw[rim:, :] = top[...].astype(F32)
    features(PAD - rim, 0, rim, raw, ids, short, mixed, queries)
    features(0, HEAD, rim, raw, ids, short, mixed, queries)
    out[HEAD:, :] = given[HEAD:, :]
    long_filter(0, HEAD, rim, ends, ids, mixed, queries, taps, skip, out, window)


def two_way(block, axis, count, hop):
    blocks, offsets, up, down = [block], [0], block, block
    for s in range(1, count // 2 + 1):
        up = lax.ppermute(up, axis, hop(1))
        blocks.append(up)
        offsets.append(-s)
        if s <= (count - 1) // 2:
            down = lax.ppermute(down, axis, hop(-1))
            blocks.append(down)
            offsets.append(s)
    return blocks, tuple(offsets)


def body(tokens, w_in, short_taps, mr_taps, skip, genome_ids):
    length, width = tokens.shape[1], tokens.shape[2]
    ctx, tp = lax.axis_size("ctx"), lax.axis_size("tp")
    xs, ys = lax.axis_size("fsdp") // ctx, ctx
    reach = mr_taps.shape[0]
    f, z, c = lax.axis_index("fsdp"), lax.axis_index("ctx"), lax.axis_index("tp")
    x, y = f % xs, f // xs

    along_x = lambda d: [(j * xs + i, j * xs + (i + d) % xs) for j in range(ys) for i in range(xs)]
    along_y = lambda d: [(j * xs + i, (j + d) % ys * xs + i) for j in range(ys) for i in range(xs)]
    along_z = lambda d: [(k, (k + d) % ctx) for k in range(ctx)]
    swap = [(0, 1), (1, 0)]

    planes = jnp.transpose(w_in, (1, 0, 2)).reshape(3, xs, tp, width, width)
    mine = lax.dynamic_index_in_dim(planes, c, 2, False).reshape(3, xs * width, width)
    theirs = lax.dynamic_index_in_dim(planes, 1 - c, 2, False).reshape(3, xs * width, width)
    mine_all = lax.all_gather(mine, "ctx", axis=0)
    theirs = lax.ppermute(theirs, "tp", swap)
    weights, weights_from = two_way(theirs, "ctx", ctx, along_z)

    own = tokens[0]
    block = jnp.zeros((xs,) + own.shape, BF16)
    block = lax.dynamic_update_index_in_dim(block, own, x, 0)
    for d in range(1, xs):
        hop = d if d <= xs // 2 else d - xs
        piece = lax.ppermute(own, "fsdp", along_x(hop))
        block = lax.dynamic_update_index_in_dim(block, piece, (x - hop) % xs, 0)
    blocks, tokens_from = two_way(block, "fsdp", ys, along_y)

    padded = jnp.pad(genome_ids[0], (LEAD, 0), constant_values=-1)
    seen = lax.dynamic_slice_in_dim(padded, z * length, length + LEAD, 0)
    ids = jnp.broadcast_to(seen[:, None], (length + LEAD, 128))
    ends = jnp.stack([seen[LEAD::GROUP], seen[LEAD + GROUP - 1 :: GROUP]], 1).reshape(-1)
    place = jnp.stack([y, z]).astype(jnp.int32)
    short = short_taps.reshape(short_taps.shape[0], -1)
    bias = skip[None, :]

    every = 2 * length * ctx * xs * width * 3 * width
    block_shape = (ys, xs, length, width)
    buffers = lambda rows: [
        pltpu.VMEM((ys, xs, rows, width), BF16),
        pltpu.VMEM((ctx,) + theirs.shape, BF16),
        pltpu.SemaphoreType.DMA((2 * ctx,)),
    ]
    give, held = call(
        functools.partial(theirs_sum, ctx, tokens_from, weights_from),
        (
            jax.ShapeDtypeStruct((length, 3 * width), BF16),
            jax.ShapeDtypeStruct(block_shape, BF16),
        ),
        [SMEM, ANY, ANY] + [HBM] * (2 * ctx),
        (VMEM, HBM),
        buffers(length) + [pltpu.SemaphoreType.DMA((ctx,))],
        flops=every,
        nbytes=8 * MIB,
        vmem=60,
    )(place, ids, ends, *blocks, *weights)
    received = lax.ppermute(give, "tp", swap)
    rim = call(
        rim_sum,
        jax.ShapeDtypeStruct((LEAD, 3 * width), BF16),
        [HBM, HBM, VMEM],
        VMEM,
        buffers(LEAD),
        flops=every * LEAD // length,
        nbytes=8 * MIB,
        vmem=60,
    )(held, mine_all, received)
    before = lax.ppermute(rim, "ctx", along_z(1))
    work = lambda rows: [
        pltpu.VMEM((rows, 3 * width), F32),
        pltpu.VMEM((rows, width), F32),
        pltpu.VMEM((length, width), F32),
        pltpu.VMEM((reach + GROUP, width), F32),
    ]
    outline = jax.ShapeDtypeStruct((length, width), BF16)
    part, top = call(
        main_part,
        (outline, jax.ShapeDtypeStruct((HEAD, 3 * width), BF16)),
        [SMEM, HBM, HBM] + [VMEM] * 5,
        (VMEM, VMEM),
        work(length) + buffers(length),
        flops=2 * every,
        nbytes=8 * MIB,
        vmem=60,
    )(ends, held, mine_all, received, ids, short, mr_taps, bias)
    gated = call(
        head_part,
        outline,
        [SMEM] + [VMEM] * 7,
        VMEM,
        work(LEAD + HEAD),
        flops=every // 4,
        nbytes=1 * MIB,
    )(ends, before, top, ids, short, mr_taps, bias, part)
    return gated[None]


def solution(mesh):
    in_specs = (
        P(None, "ctx", ("fsdp", "tp")),
        P("ctx", None, ("fsdp", "tp")),
        P(None, None, ("fsdp", "tp")),
        P(None, ("fsdp", "tp")),
        P(("fsdp", "tp")),
        P(),
    )
    out_specs = P(None, "ctx", ("fsdp", "tp"))
    return jax.shard_map(body, mesh=mesh, in_specs=in_specs, out_specs=out_specs, check_vma=False)
```

```python
import functools

import jax
import jax.numpy as jnp
from jax import lax
from jax.experimental import pallas as pl
from jax.experimental.pallas import tpu as pltpu
from jax.sharding import PartitionSpec as P

PAD = 16
LEAD = 128 + PAD
HEAD = 192
STEP = 64
CHUNK = 2
GROUP = 64
BF16, F32 = jnp.bfloat16, jnp.float32
VMEM = pl.BlockSpec(memory_space=pltpu.VMEM)
SMEM = pl.BlockSpec(memory_space=pltpu.SMEM)
ANY = pl.BlockSpec(memory_space=pl.ANY)
HBM = pl.BlockSpec(memory_space=pltpu.HBM)
MIB = 1 << 20


def call(kernel, out_shape, in_specs, out_specs, scratch=(), flops=0, nbytes=0, vmem=8):
    return pl.pallas_call(
        kernel,
        out_shape=out_shape,
        in_specs=in_specs,
        out_specs=out_specs,
        scratch_shapes=list(scratch),
        compiler_params=pltpu.CompilerParams(vmem_limit_bytes=vmem * MIB),
        cost_estimate=pl.CostEstimate(flops=flops, bytes_accessed=nbytes, transcendentals=0),
    )


def wide(planes, groups=None):
    return jnp.concatenate([planes[j] for j in range(planes.shape[0])], 1)


def fetch(pairs, sem):
    copies = [pltpu.make_async_copy(src, dst, sem.at[k]) for k, (src, dst) in enumerate(pairs)]
    for copy in copies:
        copy.start()
    return copies


def fetch(pairs, sem):
    copies = [pltpu.make_async_copy(src, dst, sem.at[k]) for k, (src, dst) in enumerate(pairs)]
    for copy in copies:
        copy.start()
    return copies


def pack(count, offsets, place, ids, ends, *refs):
    mine, other = refs[:count], refs[count : 2 * count]
    held, sem = refs[2 * count :]
    pairs = []
    for k in range(count):
        slot = lax.rem(place[0] + offsets[k] + count, count)
        pairs.append((mine[k], held.at[slot, :, place[1]]))
        pairs.append((other[k], held.at[slot, :, 1 - place[1]]))
    for copy in fetch(pairs, sem):
        copy.wait()


def project(held_in, weights_in, raw, rim, total, held, weights, sem):
    count = weights.shape[0]
    pairs = []
    for t in range(count):
        pairs.append((held_in.at[t], held.at[t]))
        pairs.append((weights_in.at[t], weights.at[t]))
    copies = fetch(pairs, sem)
    for t in range(count):
        copies[2 * t].wait()
        copies[2 * t + 1].wait()
        left = [held[t, j, c] for j in range(held.shape[1]) for c in range(held.shape[2])]
        term = jnp.dot(jnp.concatenate(left, 1), wide(weights[t]), preferred_element_type=F32)
        if t == 0:
            total[...] = term
        elif t < count - 1:
            total[...] += term
        else:
            rounded = (total[...] + term).astype(BF16)
            raw[...] = rounded
            rim[...] = rounded[rounded.shape[0] - rim.shape[0] :]


def features(first, last, shift, raw, ids, taps, mixed, queries):
    reach = taps.shape[0] - 1
    for base in range(first, last, STEP):
        step = min(STEP, last - base)
        near = ids[base + LEAD - PAD : base + LEAD + step, :]
        begin = base + shift - PAD
        sums = [jnp.zeros((step, 128), F32) for _ in range(3)]
        for g in range(3):
            if g == 0 and base < 0:
                continue
            held = raw[begin : begin + PAD + step, 128 * g : 128 * g + 128]
            for lag in range(reach + 1):
                spot = slice(PAD - lag, PAD - lag + step)
                weight = taps[lag : lag + 1, 128 * g : 128 * g + 128]
                same = near[spot] == near[PAD:]
                sums[g] = sums[g] + jnp.where(same, held[spot] * weight, 0.0)
        if base >= 0:
            queries[base : base + step, :] = sums[0]
        mixed[base + shift : base + shift + step, :] = (sums[1] * sums[2]).astype(BF16).astype(F32)


def long_filter(first, last, shift, ends, ids, mixed, queries, taps, skip, out, window):
    reach = taps.shape[0]

    def group(i, _):
        base = pl.multiple_of(first + i * GROUP, GROUP)
        here = ids[pl.ds(base + LEAD, GROUP), :]

        def genome(g, total):
            for k in range((reach + GROUP) // GROUP):
                spot = pl.ds(base + k * GROUP + LEAD - reach, GROUP)
                source = pl.ds(pl.multiple_of(base + k * GROUP + shift - reach, PAD), GROUP)
                window[k * GROUP : k * GROUP + GROUP, :] = jnp.where(
                    ids[spot, :] == g, mixed[source, :], 0.0
                )
            sums = jnp.zeros((GROUP, 128), F32)
            for s in range(8):
                held = window[8 - s : GROUP + reach - s, :]
                for a in range(reach // 8):
                    weight = taps[8 * a + s : 8 * a + s + 1, :]
                    start = reach - 8 - 8 * a
                    sums = sums + held[start : start + GROUP] * weight
            return jnp.where(here == g, sums, total)

        low, high = ends[2 * (base // GROUP)], ends[2 * (base // GROUP) + 1]
        total = lax.fori_loop(low, high + 1, genome, jnp.zeros((GROUP, 128), F32))
        bias = skip[...] * mixed[pl.ds(pl.multiple_of(base + shift, PAD), GROUP), :]
        gated = queries[pl.ds(base, GROUP), :] * (total + bias)
        out[pl.ds(base, GROUP), :] = gated.astype(out.dtype)
        return 0

    lax.fori_loop(0, (last - first) // GROUP, group, 0)


def main_part(ends, raw, ids, short, taps, skip, out, wider, mixed, queries, window):
    rows = raw.shape[0]
    wider[...] = raw[...].astype(F32)
    features(PAD, rows, 0, wider, ids, short, mixed, queries)
    long_filter(HEAD, rows, 0, ends, ids, mixed, queries, taps, skip, out, window)


def head_part(ends, before, raw, ids, short, taps, skip, given, out, wider, mixed, queries, window):
    rim = before.shape[0]
    wider[:rim, :] = before[...].astype(F32)
    wider[rim:, :] = raw[:HEAD, :].astype(F32)
    features(PAD - rim, 0, rim, wider, ids, short, mixed, queries)
    features(0, HEAD, rim, wider, ids, short, mixed, queries)
    out[HEAD:, :] = given[HEAD:, :]
    long_filter(0, HEAD, rim, ends, ids, mixed, queries, taps, skip, out, window)


def two_way(block, axis, count, hop):
    blocks, offsets, up, down = [block], [0], block, block
    for s in range(1, count // 2 + 1):
        up = lax.ppermute(up, axis, hop(1))
        blocks.append(up)
        offsets.append(-s)
        if s <= (count - 1) // 2:
            down = lax.ppermute(down, axis, hop(-1))
            blocks.append(down)
            offsets.append(s)
    return blocks, tuple(offsets)


def body(tokens, w_in, short_taps, mr_taps, skip, genome_ids):
    length, width = tokens.shape[1], tokens.shape[2]
    ctx, tp = lax.axis_size("ctx"), lax.axis_size("tp")
    xs, ys = lax.axis_size("fsdp") // ctx, ctx
    reach = mr_taps.shape[0]
    f, z, c = lax.axis_index("fsdp"), lax.axis_index("ctx"), lax.axis_index("tp")
    x, y = f % xs, f // xs

    along_x = lambda d: [(j * xs + i, j * xs + (i + d) % xs) for j in range(ys) for i in range(xs)]
    along_y = lambda d: [(j * xs + i, (j + d) % ys * xs + i) for j in range(ys) for i in range(xs)]
    along_z = lambda d: [(k, (k + d) % ctx) for k in range(ctx)]
    swap = [(0, 1), (1, 0)]

    weights = lax.all_gather(jnp.transpose(w_in, (1, 0, 2)), "ctx", axis=0)

    own = tokens[0]
    block = jnp.zeros((xs,) + own.shape, BF16)
    block = lax.dynamic_update_index_in_dim(block, own, x, 0)
    for d in range(1, xs):
        hop = d if d <= xs // 2 else d - xs
        piece = lax.ppermute(own, "fsdp", along_x(hop))
        block = lax.dynamic_update_index_in_dim(block, piece, (x - hop) % xs, 0)
    blocks, offsets = two_way(block, "fsdp", ys, along_y)
    others = [lax.ppermute(b, "tp", swap) for b in blocks]

    padded = jnp.pad(genome_ids[0], (LEAD, 0), constant_values=-1)
    seen = lax.dynamic_slice_in_dim(padded, z * length, length + LEAD, 0)
    ids = jnp.broadcast_to(seen[:, None], (length + LEAD, 128))
    ends = jnp.stack([seen[LEAD::GROUP], seen[LEAD + GROUP - 1 :: GROUP]], 1).reshape(-1)
    place = jnp.stack([y, c]).astype(jnp.int32)
    short = short_taps.reshape(short_taps.shape[0], -1)
    bias = skip[None, :]

    every = 2 * length * ctx * xs * tp * width * 3 * width
    held = call(
        functools.partial(pack, ys, offsets),
        jax.ShapeDtypeStruct((ys, xs, tp, length, width), BF16),
        [SMEM, ANY, ANY] + [ANY] * (2 * ys),
        VMEM,
        [pltpu.SemaphoreType.DMA((2 * ys,))],
        nbytes=8 * MIB,
        vmem=60,
    )(place, ids, ends, *blocks, *others)
    raw, rim = call(
        project,
        (
            jax.ShapeDtypeStruct((length, 3 * width), BF16),
            jax.ShapeDtypeStruct((LEAD, 3 * width), BF16),
        ),
        [HBM, HBM],
        (VMEM, VMEM),
        [
            pltpu.VMEM((length, 3 * width), F32),
            pltpu.VMEM(held.shape, BF16),
            pltpu.VMEM(weights.shape, BF16),
            pltpu.SemaphoreType.DMA((2 * ctx,)),
        ],
        flops=every,
        nbytes=16 * MIB,
        vmem=60,
    )(held, weights)
    before = lax.ppermute(rim, "ctx", along_z(1))
    work = lambda rows: [
        pltpu.VMEM((rows, 3 * width), F32),
        pltpu.VMEM((rows, width), F32),
        pltpu.VMEM((length, width), F32),
        pltpu.VMEM((reach + GROUP, width), F32),
    ]
    outline = jax.ShapeDtypeStruct((length, width), BF16)
    part = call(
        main_part,
        outline,
        [SMEM] + [VMEM] * 5,
        VMEM,
        work(length),
        flops=every // 2,
        nbytes=2 * MIB,
    )(ends, raw, ids, short, mr_taps, bias)
    gated = call(
        head_part,
        outline,
        [SMEM] + [VMEM] * 7,
        VMEM,
        work(LEAD + HEAD),
        flops=every // 4,
        nbytes=1 * MIB,
    )(ends, before, raw, ids, short, mr_taps, bias, part)
    return gated[None]


def solution(mesh):
    in_specs = (
        P(None, "ctx", ("fsdp", "tp")),
        P("ctx", None, ("fsdp", "tp")),
        P(None, None, ("fsdp", "tp")),
        P(None, ("fsdp", "tp")),
        P(("fsdp", "tp")),
        P(),
    )
    out_specs = P(None, "ctx", ("fsdp", "tp"))
    return jax.shard_map(body, mesh=mesh, in_specs=in_specs, out_specs=out_specs, check_vma=False)
```

```python
import functools

import jax
import jax.numpy as jnp
from jax import lax
from jax.experimental import pallas as pl
from jax.experimental.pallas import tpu as pltpu
from jax.sharding import PartitionSpec as P

PAD = 16
LEAD = 128 + PAD
HEAD = 192
STEP = 64
AHEAD = 3
VMEM_DOT = 52
GROUP = 64
BF16, F32 = jnp.bfloat16, jnp.float32
VMEM = pl.BlockSpec(memory_space=pltpu.VMEM)
SMEM = pl.BlockSpec(memory_space=pltpu.SMEM)
ANY = pl.BlockSpec(memory_space=pl.ANY)
HBM = pl.BlockSpec(memory_space=pltpu.HBM)
MIB = 1 << 20


def call(kernel, out_shape, in_specs, out_specs, scratch=(), flops=0, nbytes=0, vmem=8):
    return pl.pallas_call(
        kernel,
        out_shape=out_shape,
        in_specs=in_specs,
        out_specs=out_specs,
        scratch_shapes=list(scratch),
        compiler_params=pltpu.CompilerParams(vmem_limit_bytes=vmem * MIB),
        cost_estimate=pl.CostEstimate(flops=flops, bytes_accessed=nbytes, transcendentals=0),
    )


def wide(planes, groups=None):
    return jnp.concatenate([planes[j] for j in range(planes.shape[0])], 1)


def project(count, offsets, place, *refs):
    mine, other = refs[:count], refs[count : 2 * count]
    weights_in, raw, rim, total, held, weights, sem = refs[2 * count :]
    core = place[1]

    def copies(k):
        slot = lax.rem(place[0] + offsets[k] + count, count)
        return [
            pltpu.make_async_copy(mine[k], held.at[k, :, core], sem.at[3 * k]),
            pltpu.make_async_copy(other[k], held.at[k, :, 1 - core], sem.at[3 * k + 1]),
            pltpu.make_async_copy(weights_in.at[slot], weights.at[k], sem.at[3 * k + 2]),
        ]

    for k in range(min(AHEAD, count)):
        for copy in copies(k):
            copy.start()
    for k in range(count):
        if k + AHEAD < count:
            for copy in copies(k + AHEAD):
                copy.start()
        for copy in copies(k):
            copy.wait()
        left = [held[k, j, c] for j in range(held.shape[1]) for c in range(held.shape[2])]
        term = jnp.dot(jnp.concatenate(left, 1), wide(weights[k]), preferred_element_type=F32)
        if k == 0:
            total[...] = term
        elif k < count - 1:
            total[...] += term
        else:
            rounded = (total[...] + term).astype(BF16)
            raw[...] = rounded
            rim[...] = rounded[rounded.shape[0] - rim.shape[0] :]


def genome(place, row):
    total = (row >= place[3]).astype(jnp.int32)
    for g in (4, 5):
        total = total + (row >= place[g]).astype(jnp.int32)
    return jnp.where(row < 0, -1, total)


def fill(place, length, ids):
    row = lax.broadcasted_iota(jnp.int32, ids.shape, 0) + (place[2] * length - LEAD)
    ids[...] = genome(place, row)


def features(first, last, shift, raw, ids, taps, mixed, queries):
    reach = taps.shape[0] - 1
    for base in range(first, last, STEP):
        step = min(STEP, last - base)
        near = ids[base + LEAD - PAD : base + LEAD + step, :]
        begin = base + shift - PAD
        sums = [jnp.zeros((step, 128), F32) for _ in range(3)]
        for g in range(3):
            if g == 0 and base < 0:
                continue
            held = raw[begin : begin + PAD + step, 128 * g : 128 * g + 128]
            for lag in range(reach + 1):
                spot = slice(PAD - lag, PAD - lag + step)
                weight = taps[lag : lag + 1, 128 * g : 128 * g + 128]
                same = near[spot] == near[PAD:]
                sums[g] = sums[g] + jnp.where(same, held[spot] * weight, 0.0)
        if base >= 0:
            queries[base : base + step, :] = sums[0]
        mixed[base + shift : base + shift + step, :] = (sums[1] * sums[2]).astype(BF16).astype(F32)


def long_filter(first, last, shift, place, ids, mixed, queries, taps, skip, out, window):
    reach = taps.shape[0]

    def group(i, _):
        base = pl.multiple_of(first + i * GROUP, GROUP)
        here = ids[pl.ds(base + LEAD, GROUP), :]

        def one(g, total):
            for k in range((reach + GROUP) // GROUP):
                spot = pl.ds(base + k * GROUP + LEAD - reach, GROUP)
                source = pl.ds(pl.multiple_of(base + k * GROUP + shift - reach, PAD), GROUP)
                window[k * GROUP : k * GROUP + GROUP, :] = jnp.where(
                    ids[spot, :] == g, mixed[source, :], 0.0
                )
            sums = jnp.zeros((GROUP, 128), F32)
            for s in range(8):
                held = window[8 - s : GROUP + reach - s, :]
                for a in range(reach // 8):
                    weight = taps[8 * a + s : 8 * a + s + 1, :]
                    start = reach - 8 - 8 * a
                    sums = sums + held[start : start + GROUP] * weight
            return jnp.where(here == g, sums, total)

        row = place[2] * out.shape[0] + base
        low, high = genome(place, row), genome(place, row + GROUP - 1)
        total = lax.fori_loop(low, high + 1, one, jnp.zeros((GROUP, 128), F32))
        bias = skip[...] * mixed[pl.ds(pl.multiple_of(base + shift, PAD), GROUP), :]
        gated = queries[pl.ds(base, GROUP), :] * (total + bias)
        out[pl.ds(base, GROUP), :] = gated.astype(out.dtype)
        return 0

    lax.fori_loop(0, (last - first) // GROUP, group, 0)


def main_part(place, raw, short, taps, skip, out, wider, mixed, queries, window, ids):
    rows = raw.shape[0]
    fill(place, rows, ids)
    wider[...] = raw[...].astype(F32)
    features(PAD, rows, 0, wider, ids, short, mixed, queries)
    long_filter(HEAD, rows, 0, place, ids, mixed, queries, taps, skip, out, window)


def head_part(
    place, before, raw, short, taps, skip, given, out, wider, mixed, queries, window, ids
):
    rim = before.shape[0]
    fill(place, out.shape[0], ids)
    wider[:rim, :] = before[...].astype(F32)
    wider[rim:, :] = raw[:HEAD, :].astype(F32)
    features(PAD - rim, 0, rim, wider, ids, short, mixed, queries)
    features(0, HEAD, rim, wider, ids, short, mixed, queries)
    out[HEAD:, :] = given[HEAD:, :]
    long_filter(0, HEAD, rim, place, ids, mixed, queries, taps, skip, out, window)


def two_way(block, axis, count, hop):
    blocks, offsets, up, down = [block], [0], block, block
    for s in range(1, count // 2 + 1):
        up = lax.ppermute(up, axis, hop(1))
        blocks.append(up)
        offsets.append(-s)
        if s <= (count - 1) // 2:
            down = lax.ppermute(down, axis, hop(-1))
            blocks.append(down)
            offsets.append(s)
    return blocks, tuple(offsets)


def body(tokens, w_in, short_taps, mr_taps, skip, genome_ids):
    length, width = tokens.shape[1], tokens.shape[2]
    ctx, tp = lax.axis_size("ctx"), lax.axis_size("tp")
    xs, ys = lax.axis_size("fsdp") // ctx, ctx
    reach = mr_taps.shape[0]
    f, z, c = lax.axis_index("fsdp"), lax.axis_index("ctx"), lax.axis_index("tp")
    x, y = f % xs, f // xs

    along_x = lambda d: [(j * xs + i, j * xs + (i + d) % xs) for j in range(ys) for i in range(xs)]
    along_y = lambda d: [(j * xs + i, (j + d) % ys * xs + i) for j in range(ys) for i in range(xs)]
    swap = [(0, 1), (1, 0)]

    weights = lax.all_gather(jnp.transpose(w_in, (1, 0, 2)), "ctx", axis=0)

    own = tokens[0]
    block = jnp.zeros((xs,) + own.shape, BF16)
    block = lax.dynamic_update_index_in_dim(block, own, x, 0)
    for d in range(1, xs):
        hop = d if d <= xs // 2 else d - xs
        piece = lax.ppermute(own, "fsdp", along_x(hop))
        block = lax.dynamic_update_index_in_dim(block, piece, (x - hop) % xs, 0)
    blocks, offsets = two_way(block, "fsdp", ys, along_y)
    others = [lax.ppermute(b, "tp", swap) for b in blocks]

    starts = jnp.sum(genome_ids[0][None, :] < jnp.arange(1, 4)[:, None], axis=1, dtype=jnp.int32)
    place = jnp.concatenate([jnp.stack([y, c, z]).astype(jnp.int32), starts])
    short = short_taps.reshape(short_taps.shape[0], -1)
    bias = skip[None, :]

    every = 2 * length * ctx * xs * tp * width * 3 * width
    raw, rim = call(
        functools.partial(project, ys, offsets),
        (
            jax.ShapeDtypeStruct((length, 3 * width), BF16),
            jax.ShapeDtypeStruct((LEAD, 3 * width), BF16),
        ),
        [SMEM] + [HBM] * (2 * ys + 1),
        (VMEM, VMEM),
        [
            pltpu.VMEM((length, 3 * width), F32),
            pltpu.VMEM((ys, xs, tp, length, width), BF16),
            pltpu.VMEM(weights.shape, BF16),
            pltpu.SemaphoreType.DMA((3 * ctx,)),
        ],
        flops=every,
        nbytes=16 * MIB,
        vmem=VMEM_DOT,
    )(place, *blocks, *others, weights)
    before = lax.ppermute(rim, "ctx", [(k, k + 1) for k in range(ctx - 1)])
    work = lambda rows: [
        pltpu.VMEM((rows, 3 * width), F32),
        pltpu.VMEM((rows, width), F32),
        pltpu.VMEM((length, width), F32),
        pltpu.VMEM((reach + GROUP, width), F32),
        pltpu.VMEM((LEAD + length, width), jnp.int32),
    ]
    outline = jax.ShapeDtypeStruct((length, width), BF16)
    part = call(
        main_part,
        outline,
        [SMEM] + [VMEM] * 4,
        VMEM,
        work(length),
        flops=every // 2,
        nbytes=2 * MIB,
    )(place, raw, short, mr_taps, bias)
    gated = call(
        head_part,
        outline,
        [SMEM] + [VMEM] * 6,
        VMEM,
        work(LEAD + HEAD),
        flops=every // 4,
        nbytes=1 * MIB,
    )(place, before, raw, short, mr_taps, bias, part)
    return gated[None]


def solution(mesh):
    in_specs = (
        P(None, "ctx", ("fsdp", "tp")),
        P("ctx", None, ("fsdp", "tp")),
        P(None, None, ("fsdp", "tp")),
        P(None, ("fsdp", "tp")),
        P(("fsdp", "tp")),
        P(),
    )
    out_specs = P(None, "ctx", ("fsdp", "tp"))
    return jax.shard_map(body, mesh=mesh, in_specs=in_specs, out_specs=out_specs, check_vma=False)
```

```python
import functools

import jax
import jax.numpy as jnp
from jax import lax
from jax.experimental import pallas as pl
from jax.experimental.pallas import tpu as pltpu
from jax.sharding import PartitionSpec as P

PAD = 16
LEAD = 128 + PAD
HEAD = 192
STEP = 64
AHEAD = 3
VMEM_DOT = 52
GROUP = 64
BF16, F32 = jnp.bfloat16, jnp.float32
VMEM = pl.BlockSpec(memory_space=pltpu.VMEM)
SMEM = pl.BlockSpec(memory_space=pltpu.SMEM)
ANY = pl.BlockSpec(memory_space=pl.ANY)
HBM = pl.BlockSpec(memory_space=pltpu.HBM)
MIB = 1 << 20
COST = 20 << 30
PACE = 2


def call(kernel, out_shape, in_specs, out_specs, scratch=(), flops=0, nbytes=0, vmem=8):
    return pl.pallas_call(
        kernel,
        out_shape=out_shape,
        in_specs=in_specs,
        out_specs=out_specs,
        scratch_shapes=list(scratch),
        compiler_params=pltpu.CompilerParams(vmem_limit_bytes=vmem * MIB),
        cost_estimate=pl.CostEstimate(flops=flops, bytes_accessed=nbytes, transcendentals=0),
    )


def wide(planes, groups=None):
    return jnp.concatenate([planes[j] for j in range(planes.shape[0])], 1)


def project(count, offsets, sets, place, *refs):
    mine, other, refs = refs[: len(sets)], refs[len(sets) : 2 * len(sets)], refs[2 * len(sets) :]
    whole, halves, refs = refs[: count - 1], refs[count - 1 : count + 1], refs[count + 1 :]
    raw, rim, total, held, weights, sem = refs
    core = place[1]
    where = [(a, i) for a, size in enumerate(sets) for i in range(size)]
    half = halves[0].shape[0]

    def landing(k):
        a, i = where[k]
        return [
            pltpu.make_async_copy(mine[a].at[i], held.at[k, :, core], sem.at[4 * k]),
            pltpu.make_async_copy(other[a].at[i], held.at[k, :, 1 - core], sem.at[4 * k + 1]),
        ]

    def weight_halves(k, j):
        first, second = weights.at[k, :half], weights.at[k, half:]
        sources = halves if j == count - 1 else (whole[j].at[:half], whole[j].at[half:])
        return [
            pltpu.make_async_copy(sources[0], first, sem.at[4 * k + 2]),
            pltpu.make_async_copy(sources[1], second, sem.at[4 * k + 3]),
        ]

    def start(k):
        for copy in landing(k):
            copy.start()
        for j in range(count):
            gap = place[0] + offsets[k] - place[2] - offsets[j]

            @pl.when(lax.rem(gap + 2 * count, count) == 0)
            def _():
                for copy in weight_halves(k, j):
                    copy.start()

    for k in range(min(AHEAD, count)):
        start(k)
    for k in range(count):
        if k + AHEAD < count:
            start(k + AHEAD)
        for copy in landing(k) + weight_halves(k, count - 1):
            copy.wait()
        left = [held[k, j, c] for j in range(held.shape[1]) for c in range(held.shape[2])]
        per = weights.shape[1] // 3
        columns = [
            jnp.concatenate([weights[k, g * per + h] for h in range(per)], 0) for g in range(3)
        ]
        term = jnp.dot(
            jnp.concatenate(left, 1), jnp.concatenate(columns, 1), preferred_element_type=F32
        )
        if k == 0:
            total[...] = term
        elif k < count - 1:
            total[...] += term
        else:
            rounded = (total[...] + term).astype(BF16)
            raw[...] = rounded
            rim[...] = rounded[rounded.shape[0] - rim.shape[0] :]


def genome(place, row):
    total = (row >= place[3]).astype(jnp.int32)
    for g in (4, 5):
        total = total + (row >= place[g]).astype(jnp.int32)
    return jnp.where(row < 0, -1, total)


def fill(place, length, ids):
    row = lax.broadcasted_iota(jnp.int32, ids.shape, 0) + (place[2] * length - LEAD)
    ids[...] = genome(place, row)


def features(first, last, shift, raw, ids, taps, mixed, queries):
    reach = taps.shape[0] - 1
    for base in range(first, last, STEP):
        step = min(STEP, last - base)
        near = ids[base + LEAD - PAD : base + LEAD + step, :]
        begin = base + shift - PAD
        sums = [jnp.zeros((step, 128), F32) for _ in range(3)]
        for g in range(3):
            if g == 0 and base < 0:
                continue
            held = raw[begin : begin + PAD + step, 128 * g : 128 * g + 128]
            for lag in range(reach + 1):
                spot = slice(PAD - lag, PAD - lag + step)
                weight = taps[lag : lag + 1, 128 * g : 128 * g + 128]
                same = near[spot] == near[PAD:]
                sums[g] = sums[g] + jnp.where(same, held[spot] * weight, 0.0)
        if base >= 0:
            queries[base : base + step, :] = sums[0]
        mixed[base + shift : base + shift + step, :] = (sums[1] * sums[2]).astype(BF16).astype(F32)


def long_filter(first, last, shift, place, ids, mixed, queries, taps, skip, out, window):
    reach = taps.shape[0]

    def group(i, _):
        base = pl.multiple_of(first + i * GROUP, GROUP)
        here = ids[pl.ds(base + LEAD, GROUP), :]

        def one(g, total):
            for k in range((reach + GROUP) // GROUP):
                spot = pl.ds(base + k * GROUP + LEAD - reach, GROUP)
                source = pl.ds(pl.multiple_of(base + k * GROUP + shift - reach, PAD), GROUP)
                window[k * GROUP : k * GROUP + GROUP, :] = jnp.where(
                    ids[spot, :] == g, mixed[source, :], 0.0
                )
            sums = jnp.zeros((GROUP, 128), F32)
            for s in range(8):
                held = window[8 - s : GROUP + reach - s, :]
                for a in range(reach // 8):
                    weight = taps[8 * a + s : 8 * a + s + 1, :]
                    start = reach - 8 - 8 * a
                    sums = sums + held[start : start + GROUP] * weight
            return jnp.where(here == g, sums, total)

        row = place[2] * out.shape[0] + base
        low, high = genome(place, row), genome(place, row + GROUP - 1)
        total = lax.fori_loop(low, high + 1, one, jnp.zeros((GROUP, 128), F32))
        bias = skip[...] * mixed[pl.ds(pl.multiple_of(base + shift, PAD), GROUP), :]
        gated = queries[pl.ds(base, GROUP), :] * (total + bias)
        out[pl.ds(base, GROUP), :] = gated.astype(out.dtype)
        return 0

    lax.fori_loop(0, (last - first) // GROUP, group, 0)


def main_part(place, raw, short, taps, skip, out, wider, mixed, queries, window, ids):
    rows = raw.shape[0]
    fill(place, rows, ids)
    wider[...] = raw[...].astype(F32)
    features(PAD, rows, 0, wider, ids, short, mixed, queries)
    long_filter(HEAD, rows, 0, place, ids, mixed, queries, taps, skip, out, window)


def head_part(
    place, before, raw, short, taps, skip, given, out, wider, mixed, queries, window, ids
):
    rim = before.shape[0]
    fill(place, out.shape[0], ids)
    wider[:rim, :] = before[...].astype(F32)
    wider[rim:, :] = raw[:HEAD, :].astype(F32)
    features(PAD - rim, 0, rim, wider, ids, short, mixed, queries)
    features(0, HEAD, rim, wider, ids, short, mixed, queries)
    out[HEAD:, :] = given[HEAD:, :]
    long_filter(0, HEAD, rim, place, ids, mixed, queries, taps, skip, out, window)


def after(value, others, flops):
    def kernel(*refs):
        pass

    return pl.pallas_call(
        kernel,
        out_shape=jax.ShapeDtypeStruct(value.shape, value.dtype),
        in_specs=[ANY] * (1 + len(others)),
        out_specs=ANY,
        input_output_aliases={0: 0},
        cost_estimate=pl.CostEstimate(flops=flops, bytes_accessed=0, transcendentals=0),
    )(value, *others)


def both_ways(pair, axis, hop):
    return [lax.ppermute(pair[0], axis, hop(1)), lax.ppermute(pair[1], axis, hop(-1))]


def body(tokens, w_in, short_taps, mr_taps, skip, genome_ids):
    length, width = tokens.shape[1], tokens.shape[2]
    ctx, tp = lax.axis_size("ctx"), lax.axis_size("tp")
    xs, ys = lax.axis_size("fsdp") // ctx, ctx
    reach = mr_taps.shape[0]
    f, z, c = lax.axis_index("fsdp"), lax.axis_index("ctx"), lax.axis_index("tp")
    x, y = f % xs, f // xs

    along_x = lambda d: [(j * xs + i, j * xs + (i + d) % xs) for j in range(ys) for i in range(xs)]
    along_y = lambda d: [(j * xs + i, (j + d) % ys * xs + i) for j in range(ys) for i in range(xs)]
    swap = [(0, 1), (1, 0)]

    along_z = lambda d: [(k, (k + d) % ctx) for k in range(ctx)]
    columns = jnp.transpose(w_in, (1, 0, 2)).reshape(6, -1, width)
    weights, pair, half = [], [columns, columns], columns.shape[0] // 2
    for _ in range(1, ctx // 2):
        pair = both_ways(pair, "ctx", along_z)
        weights.append(pair)
    weights.append(both_ways([pair[0][:half], pair[1][half:]], "ctx", along_z))

    own = tokens[0]
    block = jnp.zeros((xs,) + own.shape, BF16)
    block = lax.dynamic_update_index_in_dim(block, own, x, 0)
    for d in range(1, xs):
        hop = d if d <= xs // 2 else d - xs
        piece = lax.ppermute(own, "fsdp", along_x(hop))
        block = lax.dynamic_update_index_in_dim(block, piece, (x - hop) % xs, 0)
    offsets, pair, fresh, mine, other = [0], [block, block], [block], [], []
    for r in range(1, ys // 2):
        pair = both_ways(pair, "fsdp", along_y)
        early = weights[r - 1] + other[:1] if r == 3 else weights[r - 1]
        k = 0 if r <= PACE else 1
        pair[k] = after(pair[k], early, COST)
        fresh, offsets = fresh + pair, offsets + [-r, r]
        if r in (1, ys // 2 - 1):
            mine.append(jnp.stack(fresh))
            other.append(lax.ppermute(mine[-1], "tp", swap))
            fresh = []
    final = lax.ppermute(pair[0], "fsdp", along_y(1))
    final = after(final, weights[-1], COST)
    mine.append(jnp.stack(fresh + [final]))
    other.append(lax.ppermute(mine[-1], "tp", swap))
    offsets = tuple(offsets + [-(ys // 2)])
    sets = tuple(m.shape[0] for m in mine)

    starts = jnp.sum(genome_ids[0][None, :] < jnp.arange(1, 4)[:, None], axis=1, dtype=jnp.int32)
    place = jnp.concatenate([jnp.stack([y, c, z]).astype(jnp.int32), starts])
    short = short_taps.reshape(short_taps.shape[0], -1)
    bias = skip[None, :]

    every = 2 * length * ctx * xs * tp * width * 3 * width
    raw, rim = call(
        functools.partial(project, ys, offsets, sets),
        (
            jax.ShapeDtypeStruct((length, 3 * width), BF16),
            jax.ShapeDtypeStruct((LEAD, 3 * width), BF16),
        ),
        [SMEM] + [HBM] * (2 * len(sets) + ys + 1),
        (VMEM, VMEM),
        [
            pltpu.VMEM((length, 3 * width), F32),
            pltpu.VMEM((ys, xs, tp, length, width), BF16),
            pltpu.VMEM((ctx,) + columns.shape, BF16),
            pltpu.SemaphoreType.DMA((4 * ctx,)),
        ],
        flops=every,
        nbytes=16 * MIB,
        vmem=VMEM_DOT,
    )(place, *mine, *other, columns, *[w for pair in weights for w in pair])
    before = lax.ppermute(rim, "ctx", [(k, k + 1) for k in range(ctx - 1)])
    work = lambda rows: [
        pltpu.VMEM((rows, 3 * width), F32),
        pltpu.VMEM((rows, width), F32),
        pltpu.VMEM((length, width), F32),
        pltpu.VMEM((reach + GROUP, width), F32),
        pltpu.VMEM((LEAD + length, width), jnp.int32),
    ]
    outline = jax.ShapeDtypeStruct((length, width), BF16)
    part = call(
        main_part,
        outline,
        [SMEM] + [VMEM] * 4,
        VMEM,
        work(length),
        flops=every // 2,
        nbytes=2 * MIB,
    )(place, raw, short, mr_taps, bias)
    gated = call(
        head_part,
        outline,
        [SMEM] + [VMEM] * 6,
        VMEM,
        work(LEAD + HEAD),
        flops=every // 4,
        nbytes=1 * MIB,
    )(place, before, raw, short, mr_taps, bias, part)
    return gated[None]


def solution(mesh):
    in_specs = (
        P(None, "ctx", ("fsdp", "tp")),
        P("ctx", None, ("fsdp", "tp")),
        P(None, None, ("fsdp", "tp")),
        P(None, ("fsdp", "tp")),
        P(("fsdp", "tp")),
        P(),
    )
    out_specs = P(None, "ctx", ("fsdp", "tp"))
    return jax.shard_map(body, mesh=mesh, in_specs=in_specs, out_specs=out_specs, check_vma=False)
```

```python
import functools

import jax
import jax.numpy as jnp
from jax import lax
from jax.experimental import pallas as pl
from jax.experimental.pallas import tpu as pltpu
from jax.sharding import PartitionSpec as P

PAD = 16
LEAD = 128 + PAD
HEAD = 192
STEP = 64
AHEAD = 3
VMEM_DOT = 52
GROUP = 64
BF16, F32 = jnp.bfloat16, jnp.float32
VMEM = pl.BlockSpec(memory_space=pltpu.VMEM)
SMEM = pl.BlockSpec(memory_space=pltpu.SMEM)
ANY = pl.BlockSpec(memory_space=pl.ANY)
HBM = pl.BlockSpec(memory_space=pltpu.HBM)
MIB = 1 << 20
COST = 20 << 30


def call(kernel, out_shape, in_specs, out_specs, scratch=(), flops=0, nbytes=0, vmem=8):
    return pl.pallas_call(
        kernel,
        out_shape=out_shape,
        in_specs=in_specs,
        out_specs=out_specs,
        scratch_shapes=list(scratch),
        compiler_params=pltpu.CompilerParams(vmem_limit_bytes=vmem * MIB),
        cost_estimate=pl.CostEstimate(flops=flops, bytes_accessed=nbytes, transcendentals=0),
    )


def wide(planes, groups=None):
    return jnp.concatenate([planes[j] for j in range(planes.shape[0])], 1)


def project(count, offsets, sets, place, *refs):
    mine, other, refs = refs[: len(sets)], refs[len(sets) : 2 * len(sets)], refs[2 * len(sets) :]
    parts, refs = refs[:count], refs[count:]
    raw, rim, total, held, weights, sem = refs
    core = place[1]
    where = [(a, i) for a, size in enumerate(sets) for i in range(size)]
    sign = 1 - 2 * core

    def landing(k):
        a, i = where[k]
        b, j = where[offsets.index(-offsets[k])] if 0 < k < count - 1 else where[k]
        return [
            pltpu.make_async_copy(mine[a].at[i], held.at[k, :, core], sem.at[4 * k]),
            pltpu.make_async_copy(other[b].at[j], held.at[k, :, 1 - core], sem.at[4 * k + 1]),
        ]

    def panel(k, j):
        return pltpu.make_async_copy(parts[j], weights.at[k], sem.at[4 * k + 2])

    def start(k):
        for copy in landing(k):
            copy.start()
        for j in range(count):
            gap = place[0] - place[2] + sign * (offsets[k] - offsets[j])

            @pl.when(lax.rem(gap + 2 * count, count) == 0)
            def _():
                panel(k, j).start()

    for k in range(min(AHEAD, count)):
        start(k)
    for k in range(count):
        if k + AHEAD < count:
            start(k + AHEAD)
        for copy in landing(k) + [panel(k, 0)]:
            copy.wait()
        left = [held[k, j, c] for j in range(held.shape[1]) for c in range(held.shape[2])]
        term = jnp.dot(jnp.concatenate(left, 1), wide(weights[k]), preferred_element_type=F32)
        if k == 0:
            total[...] = term
        elif k < count - 1:
            total[...] += term
        else:
            rounded = (total[...] + term).astype(BF16)
            raw[...] = rounded
            rim[...] = rounded[rounded.shape[0] - rim.shape[0] :]


def genome(place, row):
    total = (row >= place[3]).astype(jnp.int32)
    for g in (4, 5):
        total = total + (row >= place[g]).astype(jnp.int32)
    return jnp.where(row < 0, -1, total)


def fill(place, length, ids):
    row = lax.broadcasted_iota(jnp.int32, ids.shape, 0) + (place[2] * length - LEAD)
    ids[...] = genome(place, row)


def features(first, last, shift, raw, ids, taps, mixed, queries):
    reach = taps.shape[0] - 1
    for base in range(first, last, STEP):
        step = min(STEP, last - base)
        near = ids[base + LEAD - PAD : base + LEAD + step, :]
        begin = base + shift - PAD
        sums = [jnp.zeros((step, 128), F32) for _ in range(3)]
        for g in range(3):
            if g == 0 and base < 0:
                continue
            held = raw[begin : begin + PAD + step, 128 * g : 128 * g + 128]
            for lag in range(reach + 1):
                spot = slice(PAD - lag, PAD - lag + step)
                weight = taps[lag : lag + 1, 128 * g : 128 * g + 128]
                same = near[spot] == near[PAD:]
                sums[g] = sums[g] + jnp.where(same, held[spot] * weight, 0.0)
        if base >= 0:
            queries[base : base + step, :] = sums[0]
        mixed[base + shift : base + shift + step, :] = (sums[1] * sums[2]).astype(BF16).astype(F32)


def long_filter(first, last, shift, place, ids, mixed, queries, taps, skip, out, window):
    reach = taps.shape[0]

    def group(i, _):
        base = pl.multiple_of(first + i * GROUP, GROUP)
        here = ids[pl.ds(base + LEAD, GROUP), :]

        def one(g, total):
            for k in range((reach + GROUP) // GROUP):
                spot = pl.ds(base + k * GROUP + LEAD - reach, GROUP)
                source = pl.ds(pl.multiple_of(base + k * GROUP + shift - reach, PAD), GROUP)
                window[k * GROUP : k * GROUP + GROUP, :] = jnp.where(
                    ids[spot, :] == g, mixed[source, :], 0.0
                )
            sums = jnp.zeros((GROUP, 128), F32)
            for s in range(8):
                held = window[8 - s : GROUP + reach - s, :]
                for a in range(reach // 8):
                    weight = taps[8 * a + s : 8 * a + s + 1, :]
                    start = reach - 8 - 8 * a
                    sums = sums + held[start : start + GROUP] * weight
            return jnp.where(here == g, sums, total)

        row = place[2] * out.shape[0] + base
        low, high = genome(place, row), genome(place, row + GROUP - 1)
        total = lax.fori_loop(low, high + 1, one, jnp.zeros((GROUP, 128), F32))
        bias = skip[...] * mixed[pl.ds(pl.multiple_of(base + shift, PAD), GROUP), :]
        gated = queries[pl.ds(base, GROUP), :] * (total + bias)
        out[pl.ds(base, GROUP), :] = gated.astype(out.dtype)
        return 0

    lax.fori_loop(0, (last - first) // GROUP, group, 0)


def main_part(place, raw, short, taps, skip, out, wider, mixed, queries, window, ids):
    rows = raw.shape[0]
    fill(place, rows, ids)
    wider[...] = raw[...].astype(F32)
    features(PAD, rows, 0, wider, ids, short, mixed, queries)
    long_filter(HEAD, rows, 0, place, ids, mixed, queries, taps, skip, out, window)


def head_part(
    place, before, raw, short, taps, skip, given, out, wider, mixed, queries, window, ids
):
    rim = before.shape[0]
    fill(place, out.shape[0], ids)
    wider[:rim, :] = before[...].astype(F32)
    wider[rim:, :] = raw[:HEAD, :].astype(F32)
    features(PAD - rim, 0, rim, wider, ids, short, mixed, queries)
    features(0, HEAD, rim, wider, ids, short, mixed, queries)
    out[HEAD:, :] = given[HEAD:, :]
    long_filter(0, HEAD, rim, place, ids, mixed, queries, taps, skip, out, window)


def after(value, others, flops):
    def kernel(*refs):
        pass

    return pl.pallas_call(
        kernel,
        out_shape=jax.ShapeDtypeStruct(value.shape, value.dtype),
        in_specs=[ANY] * (1 + len(others)),
        out_specs=ANY,
        input_output_aliases={0: 0},
        cost_estimate=pl.CostEstimate(flops=flops, bytes_accessed=0, transcendentals=0),
    )(value, *others)


def both_ways(pair, axis, first, second):
    return [lax.ppermute(pair[0], axis, first), lax.ppermute(pair[1], axis, second)]


def body(tokens, w_in, short_taps, mr_taps, skip, genome_ids):
    length, width = tokens.shape[1], tokens.shape[2]
    ctx, tp = lax.axis_size("ctx"), lax.axis_size("tp")
    xs, ys = lax.axis_size("fsdp") // ctx, ctx
    reach = mr_taps.shape[0]
    f, z, c = lax.axis_index("fsdp"), lax.axis_index("ctx"), lax.axis_index("tp")
    x, y = f % xs, f // xs

    along_x = lambda d: [(j * xs + i, j * xs + (i + d) % xs) for j in range(ys) for i in range(xs)]
    along_y = lambda d: [
        ((j * xs + i) * tp + t, ((j + d - 2 * d * t) % ys * xs + i) * tp + t)
        for j in range(ys) for i in range(xs) for t in range(tp)
    ]
    along_z = lambda d: [
        (k * tp + t, (k + d - 2 * d * t) % ctx * tp + t) for k in range(ctx) for t in range(tp)
    ]
    on_y, on_z = ("fsdp", "tp"), ("ctx", "tp")
    swap = [(0, 1), (1, 0)]

    columns = jnp.transpose(w_in, (1, 0, 2))
    weights, pair = [], [columns, columns]
    for _ in range(1, ctx // 2):
        pair = both_ways(pair, on_z, along_z(1), along_z(-1))
        weights.append(pair)
    weights.append([lax.ppermute(pair[0], on_z, along_z(1))])

    own = tokens[0]
    block = jnp.zeros((xs,) + own.shape, BF16)
    block = lax.dynamic_update_index_in_dim(block, own, x, 0)
    for d in range(1, xs):
        hop = d if d <= xs // 2 else d - xs
        piece = lax.ppermute(own, "fsdp", along_x(hop))
        block = lax.dynamic_update_index_in_dim(block, piece, (x - hop) % xs, 0)
    offsets, pair, fresh, mine, other = [0], [block, block], [block], [], []
    for r in range(1, ys // 2):
        pair = both_ways(pair, on_y, along_y(1), along_y(-1))
        early = weights[r - 1] + other[:1] if r == 3 else weights[r - 1]
        k = 0 if r <= 2 else 1
        pair[k] = after(pair[k], early, COST)
        fresh, offsets = fresh + pair, offsets + [-r, r]
        if r in (1, ys // 2 - 1):
            mine.append(jnp.stack(fresh))
            other.append(lax.ppermute(mine[-1], "tp", swap))
            fresh = []
    final = lax.ppermute(pair[0], on_y, along_y(1))
    crossed = lax.ppermute(pair[0], on_y, [(i, j // tp * tp + 1 - j % tp) for i, j in along_y(1)])
    final = after(final, weights[-1], COST)
    if fresh:
        mine.append(jnp.stack(fresh))
        other.append(lax.ppermute(mine[-1], "tp", swap))
    mine.append(final[None])
    other.append(crossed[None])
    offsets = tuple(offsets + [-(ys // 2)])
    sets = tuple(m.shape[0] for m in mine)

    starts = jnp.sum(genome_ids[0][None, :] < jnp.arange(1, 4)[:, None], axis=1, dtype=jnp.int32)
    place = jnp.concatenate([jnp.stack([y, c, z]).astype(jnp.int32), starts])
    short = short_taps.reshape(short_taps.shape[0], -1)
    bias = skip[None, :]

    every = 2 * length * ctx * xs * tp * width * 3 * width
    raw, rim = call(
        functools.partial(project, ys, offsets, sets),
        (
            jax.ShapeDtypeStruct((length, 3 * width), BF16),
            jax.ShapeDtypeStruct((LEAD, 3 * width), BF16),
        ),
        [SMEM] + [HBM] * (2 * len(sets) + ys),
        (VMEM, VMEM),
        [
            pltpu.VMEM((length, 3 * width), F32),
            pltpu.VMEM((ys, xs, tp, length, width), BF16),
            pltpu.VMEM((ctx,) + columns.shape, BF16),
            pltpu.SemaphoreType.DMA((4 * ctx,)),
        ],
        flops=every,
        nbytes=16 * MIB,
        vmem=VMEM_DOT,
    )(place, *mine, *other, columns, *[w for pair in weights for w in pair])
    before = lax.ppermute(rim, "ctx", [(k, k + 1) for k in range(ctx - 1)])
    work = lambda rows: [
        pltpu.VMEM((rows, 3 * width), F32),
        pltpu.VMEM((rows, width), F32),
        pltpu.VMEM((length, width), F32),
        pltpu.VMEM((reach + GROUP, width), F32),
        pltpu.VMEM((LEAD + length, width), jnp.int32),
    ]
    outline = jax.ShapeDtypeStruct((length, width), BF16)
    part = call(
        main_part,
        outline,
        [SMEM] + [VMEM] * 4,
        VMEM,
        work(length),
        flops=every // 2,
        nbytes=2 * MIB,
    )(place, raw, short, mr_taps, bias)
    gated = call(
        head_part,
        outline,
        [SMEM] + [VMEM] * 6,
        VMEM,
        work(LEAD + HEAD),
        flops=every // 4,
        nbytes=1 * MIB,
    )(place, before, raw, short, mr_taps, bias, part)
    return gated[None]


def solution(mesh):
    in_specs = (
        P(None, "ctx", ("fsdp", "tp")),
        P("ctx", None, ("fsdp", "tp")),
        P(None, None, ("fsdp", "tp")),
        P(None, ("fsdp", "tp")),
        P(("fsdp", "tp")),
        P(),
    )
    out_specs = P(None, "ctx", ("fsdp", "tp"))
    return jax.shard_map(body, mesh=mesh, in_specs=in_specs, out_specs=out_specs, check_vma=False)
```

```python
import functools

import jax
import jax.numpy as jnp
from jax import lax
from jax.experimental import pallas as pl
from jax.experimental.pallas import tpu as pltpu
from jax.sharding import PartitionSpec as P

PAD = 16
LEAD = 128 + PAD
HEAD = 192
STEP = 64
AHEAD = 3
VMEM_DOT = 52
GROUP = 64
BF16, F32 = jnp.bfloat16, jnp.float32
VMEM = pl.BlockSpec(memory_space=pltpu.VMEM)
SMEM = pl.BlockSpec(memory_space=pltpu.SMEM)
ANY = pl.BlockSpec(memory_space=pl.ANY)
HBM = pl.BlockSpec(memory_space=pltpu.HBM)
MIB = 1 << 20
COST = 5 << 30


def call(kernel, out_shape, in_specs, out_specs, scratch=(), flops=0, nbytes=0, vmem=8):
    return pl.pallas_call(
        kernel,
        out_shape=out_shape,
        in_specs=in_specs,
        out_specs=out_specs,
        scratch_shapes=list(scratch),
        compiler_params=pltpu.CompilerParams(vmem_limit_bytes=vmem * MIB),
        cost_estimate=pl.CostEstimate(flops=flops, bytes_accessed=nbytes, transcendentals=0),
    )


def wide(planes, groups=None):
    return jnp.concatenate([planes[j] for j in range(planes.shape[0])], 1)


def project(count, offsets, sets, place, *refs):
    mine, other, refs = refs[: len(sets)], refs[len(sets) : 2 * len(sets)], refs[2 * len(sets) :]
    parts, refs = refs[:count], refs[count:]
    gathered, raw, rim, total, held, weights, sem = refs
    core = place[1]
    where = [(a, i) for a, size in enumerate(sets) for i in range(size)]
    sign = 1 - 2 * core

    def landing(k):
        a, i = where[k]
        b, j = where[offsets.index(-offsets[k])] if 0 < k < count - 1 else where[k]
        return [
            pltpu.make_async_copy(mine[a].at[i], held.at[k, :, core], sem.at[4 * k]),
            pltpu.make_async_copy(other[b].at[j], held.at[k, :, 1 - core], sem.at[4 * k + 1]),
        ]

    def panel(k, j):
        return pltpu.make_async_copy(parts[j], weights.at[k, 0], sem.at[4 * k + 2])

    def others(k):
        slot = lax.rem(place[0] + sign * offsets[k] + count, count)
        return pltpu.make_async_copy(gathered.at[slot], weights.at[k, 1:], sem.at[4 * k + 3])

    def start(k):
        for copy in landing(k) + [others(k)]:
            copy.start()
        for j in range(count):
            gap = place[0] - place[2] + sign * (offsets[k] - offsets[j])

            @pl.when(lax.rem(gap + 2 * count, count) == 0)
            def _():
                panel(k, j).start()

    for k in range(min(AHEAD, count)):
        start(k)
    for k in range(count):
        if k + AHEAD < count:
            start(k + AHEAD)
        for copy in landing(k) + [others(k), panel(k, 0)]:
            copy.wait()
        left = [held[k, j, c] for j in range(held.shape[1]) for c in range(held.shape[2])]
        term = jnp.dot(jnp.concatenate(left, 1), wide(weights[k]), preferred_element_type=F32)
        if k == 0:
            total[...] = term
        elif k < count - 1:
            total[...] += term
        else:
            rounded = (total[...] + term).astype(BF16)
            raw[...] = rounded
            rim[...] = rounded[rounded.shape[0] - rim.shape[0] :]


def genome(place, row):
    total = (row >= place[3]).astype(jnp.int32)
    for g in (4, 5):
        total = total + (row >= place[g]).astype(jnp.int32)
    return jnp.where(row < 0, -1, total)


def fill(place, length, ids):
    row = lax.broadcasted_iota(jnp.int32, ids.shape, 0) + (place[2] * length - LEAD)
    ids[...] = genome(place, row)


def features(first, last, shift, raw, ids, taps, mixed, queries):
    reach = taps.shape[0] - 1
    for base in range(first, last, STEP):
        step = min(STEP, last - base)
        near = ids[base + LEAD - PAD : base + LEAD + step, :]
        begin = base + shift - PAD
        sums = [jnp.zeros((step, 128), F32) for _ in range(3)]
        for g in range(3):
            if g == 0 and base < 0:
                continue
            held = raw[begin : begin + PAD + step, 128 * g : 128 * g + 128]
            for lag in range(reach + 1):
                spot = slice(PAD - lag, PAD - lag + step)
                weight = taps[lag : lag + 1, 128 * g : 128 * g + 128]
                same = near[spot] == near[PAD:]
                sums[g] = sums[g] + jnp.where(same, held[spot] * weight, 0.0)
        if base >= 0:
            queries[base : base + step, :] = sums[0]
        mixed[base + shift : base + shift + step, :] = (sums[1] * sums[2]).astype(BF16).astype(F32)


def long_filter(first, last, shift, place, ids, mixed, queries, taps, skip, out, window):
    reach = taps.shape[0]

    def group(i, _):
        base = pl.multiple_of(first + i * GROUP, GROUP)
        here = ids[pl.ds(base + LEAD, GROUP), :]

        def one(g, total):
            for k in range((reach + GROUP) // GROUP):
                spot = pl.ds(base + k * GROUP + LEAD - reach, GROUP)
                source = pl.ds(pl.multiple_of(base + k * GROUP + shift - reach, PAD), GROUP)
                window[k * GROUP : k * GROUP + GROUP, :] = jnp.where(
                    ids[spot, :] == g, mixed[source, :], 0.0
                )
            sums = jnp.zeros((GROUP, 128), F32)
            for s in range(8):
                held = window[8 - s : GROUP + reach - s, :]
                for a in range(reach // 8):
                    weight = taps[8 * a + s : 8 * a + s + 1, :]
                    start = reach - 8 - 8 * a
                    sums = sums + held[start : start + GROUP] * weight
            return jnp.where(here == g, sums, total)

        row = place[2] * out.shape[0] + base
        low, high = genome(place, row), genome(place, row + GROUP - 1)
        total = lax.fori_loop(low, high + 1, one, jnp.zeros((GROUP, 128), F32))
        bias = skip[...] * mixed[pl.ds(pl.multiple_of(base + shift, PAD), GROUP), :]
        gated = queries[pl.ds(base, GROUP), :] * (total + bias)
        out[pl.ds(base, GROUP), :] = gated.astype(out.dtype)
        return 0

    lax.fori_loop(0, (last - first) // GROUP, group, 0)


def main_part(place, raw, short, taps, skip, out, wider, mixed, queries, window, ids):
    rows = raw.shape[0]
    fill(place, rows, ids)
    wider[...] = raw[...].astype(F32)
    features(PAD, rows, 0, wider, ids, short, mixed, queries)
    long_filter(HEAD, rows, 0, place, ids, mixed, queries, taps, skip, out, window)


def head_part(
    place, before, raw, short, taps, skip, given, out, wider, mixed, queries, window, ids
):
    rim = before.shape[0]
    fill(place, out.shape[0], ids)
    wider[:rim, :] = before[...].astype(F32)
    wider[rim:, :] = raw[:HEAD, :].astype(F32)
    features(PAD - rim, 0, rim, wider, ids, short, mixed, queries)
    features(0, HEAD, rim, wider, ids, short, mixed, queries)
    out[HEAD:, :] = given[HEAD:, :]
    long_filter(0, HEAD, rim, place, ids, mixed, queries, taps, skip, out, window)


def after(value, others, flops):
    def kernel(*refs):
        pass

    return pl.pallas_call(
        kernel,
        out_shape=jax.ShapeDtypeStruct(value.shape, value.dtype),
        in_specs=[ANY] * (1 + len(others)),
        out_specs=ANY,
        input_output_aliases={0: 0},
        cost_estimate=pl.CostEstimate(flops=flops, bytes_accessed=0, transcendentals=0),
    )(value, *others)


def both_ways(pair, axis, first, second):
    return [lax.ppermute(pair[0], axis, first), lax.ppermute(pair[1], axis, second)]


def body(tokens, w_in, short_taps, mr_taps, skip, genome_ids):
    length, width = tokens.shape[1], tokens.shape[2]
    ctx, tp = lax.axis_size("ctx"), lax.axis_size("tp")
    xs, ys = lax.axis_size("fsdp") // ctx, ctx
    reach = mr_taps.shape[0]
    f, z, c = lax.axis_index("fsdp"), lax.axis_index("ctx"), lax.axis_index("tp")
    x, y = f % xs, f // xs

    along_x = lambda d: [(j * xs + i, j * xs + (i + d) % xs) for j in range(ys) for i in range(xs)]
    along_y = lambda d: [
        ((j * xs + i) * tp + t, ((j + d - 2 * d * t) % ys * xs + i) * tp + t)
        for j in range(ys) for i in range(xs) for t in range(tp)
    ]
    along_z = lambda d: [
        (k * tp + t, (k + d - 2 * d * t) % ctx * tp + t) for k in range(ctx) for t in range(tp)
    ]
    on_y, on_z = ("fsdp", "tp"), ("ctx", "tp")
    swap = [(0, 1), (1, 0)]

    planes = jnp.transpose(w_in, (1, 0, 2))
    gathered = lax.all_gather(planes[1:], "ctx", axis=0)
    columns = planes[0]
    weights, pair = [], [columns, columns]
    for _ in range(1, ctx // 2):
        pair = both_ways(pair, on_z, along_z(1), along_z(-1))
        weights.append(pair)
    weights.append([lax.ppermute(pair[0], on_z, along_z(1))])

    own = tokens[0]
    block = jnp.zeros((xs,) + own.shape, BF16)
    block = lax.dynamic_update_index_in_dim(block, own, x, 0)
    for d in range(1, xs):
        hop = d if d <= xs // 2 else d - xs
        piece = lax.ppermute(own, "fsdp", along_x(hop))
        block = lax.dynamic_update_index_in_dim(block, piece, (x - hop) % xs, 0)
    offsets, pair, fresh, mine, other = [0], [block, block], [block], [], []
    for r in range(1, ys // 2):
        pair = both_ways(pair, on_y, along_y(1), along_y(-1))
        early = weights[r - 1] + other[:1] if r == 3 else weights[r - 1]
        k = 0 if r <= 2 else 1
        pair[k] = after(pair[k], early, COST)
        fresh, offsets = fresh + pair, offsets + [-r, r]
        if r in (1, ys // 2 - 1):
            mine.append(jnp.stack(fresh))
            other.append(lax.ppermute(mine[-1], "tp", swap))
            fresh = []
    final = lax.ppermute(pair[0], on_y, along_y(1))
    crossed = lax.ppermute(pair[0], on_y, [(i, j // tp * tp + 1 - j % tp) for i, j in along_y(1)])
    final = after(final, weights[-1], COST)
    if fresh:
        mine.append(jnp.stack(fresh))
        other.append(lax.ppermute(mine[-1], "tp", swap))
    mine.append(final[None])
    other.append(crossed[None])
    offsets = tuple(offsets + [-(ys // 2)])
    sets = tuple(m.shape[0] for m in mine)

    starts = jnp.sum(genome_ids[0][None, :] < jnp.arange(1, 4)[:, None], axis=1, dtype=jnp.int32)
    place = jnp.concatenate([jnp.stack([y, c, z]).astype(jnp.int32), starts])
    short = short_taps.reshape(short_taps.shape[0], -1)
    bias = skip[None, :]

    every = 2 * length * ctx * xs * tp * width * 3 * width
    raw, rim = call(
        functools.partial(project, ys, offsets, sets),
        (
            jax.ShapeDtypeStruct((length, 3 * width), BF16),
            jax.ShapeDtypeStruct((LEAD, 3 * width), BF16),
        ),
        [SMEM] + [HBM] * (2 * len(sets) + ys + 1),
        (VMEM, VMEM),
        [
            pltpu.VMEM((length, 3 * width), F32),
            pltpu.VMEM((ys, xs, tp, length, width), BF16),
            pltpu.VMEM((ctx,) + planes.shape, BF16),
            pltpu.SemaphoreType.DMA((4 * ctx,)),
        ],
        flops=every,
        nbytes=16 * MIB,
        vmem=VMEM_DOT,
    )(place, *mine, *other, columns, *[w for pair in weights for w in pair], gathered)
    before = lax.ppermute(rim, "ctx", [(k, k + 1) for k in range(ctx - 1)])
    work = lambda rows: [
        pltpu.VMEM((rows, 3 * width), F32),
        pltpu.VMEM((rows, width), F32),
        pltpu.VMEM((length, width), F32),
        pltpu.VMEM((reach + GROUP, width), F32),
        pltpu.VMEM((LEAD + length, width), jnp.int32),
    ]
    outline = jax.ShapeDtypeStruct((length, width), BF16)
    part = call(
        main_part,
        outline,
        [SMEM] + [VMEM] * 4,
        VMEM,
        work(length),
        flops=every // 2,
        nbytes=2 * MIB,
    )(place, raw, short, mr_taps, bias)
    gated = call(
        head_part,
        outline,
        [SMEM] + [VMEM] * 6,
        VMEM,
        work(LEAD + HEAD),
        flops=every // 4,
        nbytes=1 * MIB,
    )(place, before, raw, short, mr_taps, bias, part)
    return gated[None]


def solution(mesh):
    in_specs = (
        P(None, "ctx", ("fsdp", "tp")),
        P("ctx", None, ("fsdp", "tp")),
        P(None, None, ("fsdp", "tp")),
        P(None, ("fsdp", "tp")),
        P(("fsdp", "tp")),
        P(),
    )
    out_specs = P(None, "ctx", ("fsdp", "tp"))
    return jax.shard_map(body, mesh=mesh, in_specs=in_specs, out_specs=out_specs, check_vma=False)
```

```python
import functools

import jax
import jax.numpy as jnp
from jax import lax
from jax.experimental import pallas as pl
from jax.experimental.pallas import tpu as pltpu
from jax.sharding import PartitionSpec as P

PAD = 16
LEAD = 128 + PAD
HEAD = 192
STEP = 64
AHEAD = 3
VMEM_DOT = 52
GROUP = 64
BF16, F32 = jnp.bfloat16, jnp.float32
VMEM = pl.BlockSpec(memory_space=pltpu.VMEM)
SMEM = pl.BlockSpec(memory_space=pltpu.SMEM)
ANY = pl.BlockSpec(memory_space=pl.ANY)
HBM = pl.BlockSpec(memory_space=pltpu.HBM)
MIB = 1 << 20


def call(kernel, out_shape, in_specs, out_specs, scratch=(), flops=0, nbytes=0, vmem=8):
    return pl.pallas_call(
        kernel,
        out_shape=out_shape,
        in_specs=in_specs,
        out_specs=out_specs,
        scratch_shapes=list(scratch),
        compiler_params=pltpu.CompilerParams(vmem_limit_bytes=vmem * MIB),
        cost_estimate=pl.CostEstimate(flops=flops, bytes_accessed=nbytes, transcendentals=0),
    )


def wide(planes, groups=None):
    return jnp.concatenate([planes[j] for j in range(planes.shape[0])], 1)


def project(count, offsets, place, *refs):
    mine, other = refs[:count], refs[count : 2 * count]
    weights_in, raw, rim, total, held, weights, sem = refs[2 * count :]
    core = place[1]

    def copies(k):
        slot = lax.rem(place[0] + offsets[k] + count, count)
        return [
            pltpu.make_async_copy(mine[k], held.at[k, :, core], sem.at[3 * k]),
            pltpu.make_async_copy(other[k], held.at[k, :, 1 - core], sem.at[3 * k + 1]),
            pltpu.make_async_copy(weights_in.at[slot], weights.at[k], sem.at[3 * k + 2]),
        ]

    for k in range(min(AHEAD, count)):
        for copy in copies(k):
            copy.start()
    for k in range(count):
        if k + AHEAD < count:
            for copy in copies(k + AHEAD):
                copy.start()
        for copy in copies(k):
            copy.wait()
        left = [held[k, j, c] for j in range(held.shape[1]) for c in range(held.shape[2])]
        term = jnp.dot(jnp.concatenate(left, 1), wide(weights[k]), preferred_element_type=F32)
        if k == 0:
            total[...] = term
        elif k < count - 1:
            total[...] += term
        else:
            rounded = (total[...] + term).astype(BF16)
            raw[...] = rounded
            rim[...] = rounded[rounded.shape[0] - rim.shape[0] :]


def genome(place, row):
    total = (row >= place[3]).astype(jnp.int32)
    for g in (4, 5):
        total = total + (row >= place[g]).astype(jnp.int32)
    return jnp.where(row < 0, -1, total)


def fill(place, length, ids):
    row = lax.broadcasted_iota(jnp.int32, ids.shape, 0) + (place[2] * length - LEAD)
    ids[...] = genome(place, row)


def features(first, last, shift, raw, ids, taps, mixed, queries):
    reach = taps.shape[0] - 1
    for base in range(first, last, STEP):
        step = min(STEP, last - base)
        near = ids[base + LEAD - PAD : base + LEAD + step, :]
        begin = base + shift - PAD
        sums = [jnp.zeros((step, 128), F32) for _ in range(3)]
        for g in range(3):
            if g == 0 and base < 0:
                continue
            held = raw[begin : begin + PAD + step, 128 * g : 128 * g + 128]
            for lag in range(reach + 1):
                spot = slice(PAD - lag, PAD - lag + step)
                weight = taps[lag : lag + 1, 128 * g : 128 * g + 128]
                same = near[spot] == near[PAD:]
                sums[g] = sums[g] + jnp.where(same, held[spot] * weight, 0.0)
        if base >= 0:
            queries[base : base + step, :] = sums[0]
        mixed[base + shift : base + shift + step, :] = (sums[1] * sums[2]).astype(BF16).astype(F32)


def long_filter(first, last, shift, place, ids, mixed, queries, taps, skip, out, window):
    reach = taps.shape[0]

    def group(i, _):
        base = pl.multiple_of(first + i * GROUP, GROUP)
        here = ids[pl.ds(base + LEAD, GROUP), :]

        def one(g, total):
            for k in range((reach + GROUP) // GROUP):
                spot = pl.ds(base + k * GROUP + LEAD - reach, GROUP)
                source = pl.ds(pl.multiple_of(base + k * GROUP + shift - reach, PAD), GROUP)
                window[k * GROUP : k * GROUP + GROUP, :] = jnp.where(
                    ids[spot, :] == g, mixed[source, :], 0.0
                )
            sums = jnp.zeros((GROUP, 128), F32)
            for s in range(8):
                held = window[8 - s : GROUP + reach - s, :]
                for a in range(reach // 8):
                    weight = taps[8 * a + s : 8 * a + s + 1, :]
                    start = reach - 8 - 8 * a
                    sums = sums + held[start : start + GROUP] * weight
            return jnp.where(here == g, sums, total)

        row = place[2] * out.shape[0] + base
        low, high = genome(place, row), genome(place, row + GROUP - 1)
        total = lax.fori_loop(low, high + 1, one, jnp.zeros((GROUP, 128), F32))
        bias = skip[...] * mixed[pl.ds(pl.multiple_of(base + shift, PAD), GROUP), :]
        gated = queries[pl.ds(base, GROUP), :] * (total + bias)
        out[pl.ds(base, GROUP), :] = gated.astype(out.dtype)
        return 0

    lax.fori_loop(0, (last - first) // GROUP, group, 0)


def main_part(
    place, raw, short, taps, skip, out, top_mixed, top_queries, wider, mixed, queries, window, ids
):
    rows = raw.shape[0]
    fill(place, rows, ids)
    wider[...] = raw[...].astype(F32)
    features(PAD, rows, 0, wider, ids, short, mixed, queries)
    top_mixed[...] = mixed[PAD:HEAD, :]
    top_queries[...] = queries[PAD:HEAD, :]
    long_filter(HEAD, rows, 0, place, ids, mixed, queries, taps, skip, out, window)


def head_part(
    place, before, raw, short, taps, skip, given, top_mixed, top_queries,
    out, wider, mixed, queries, window, ids,
):
    rim = before.shape[0]
    fill(place, out.shape[0], ids)
    wider[:rim, :] = before[...].astype(F32)
    wider[rim:, :] = raw[:PAD, :].astype(F32)
    features(PAD - rim, 0, rim, wider, ids, short, mixed, queries)
    features(0, PAD, rim, wider, ids, short, mixed, queries)
    mixed[rim + PAD :, :] = top_mixed[...]
    queries[PAD:HEAD, :] = top_queries[...]
    out[HEAD:, :] = given[HEAD:, :]
    long_filter(0, HEAD, rim, place, ids, mixed, queries, taps, skip, out, window)


def two_way(block, axis, count, hop):
    blocks, offsets, up, down = [block], [0], block, block
    for s in range(1, count // 2 + 1):
        up = lax.ppermute(up, axis, hop(1))
        blocks.append(up)
        offsets.append(-s)
        if s <= (count - 1) // 2:
            down = lax.ppermute(down, axis, hop(-1))
            blocks.append(down)
            offsets.append(s)
    return blocks, tuple(offsets)


def body(tokens, w_in, short_taps, mr_taps, skip, genome_ids):
    length, width = tokens.shape[1], tokens.shape[2]
    ctx, tp = lax.axis_size("ctx"), lax.axis_size("tp")
    xs, ys = lax.axis_size("fsdp") // ctx, ctx
    reach = mr_taps.shape[0]
    f, z, c = lax.axis_index("fsdp"), lax.axis_index("ctx"), lax.axis_index("tp")
    x, y = f % xs, f // xs

    along_x = lambda d: [(j * xs + i, j * xs + (i + d) % xs) for j in range(ys) for i in range(xs)]
    along_y = lambda d: [(j * xs + i, (j + d) % ys * xs + i) for j in range(ys) for i in range(xs)]
    swap = [(0, 1), (1, 0)]

    weights = lax.all_gather(jnp.transpose(w_in, (1, 0, 2)), "ctx", axis=0)

    own = tokens[0]
    block = jnp.zeros((xs,) + own.shape, BF16)
    block = lax.dynamic_update_index_in_dim(block, own, x, 0)
    for d in range(1, xs):
        hop = d if d <= xs // 2 else d - xs
        piece = lax.ppermute(own, "fsdp", along_x(hop))
        block = lax.dynamic_update_index_in_dim(block, piece, (x - hop) % xs, 0)
    blocks, offsets = two_way(block, "fsdp", ys, along_y)
    others = [lax.ppermute(b, "tp", swap) for b in blocks]

    starts = jnp.sum(genome_ids[0][None, :] < jnp.arange(1, 4)[:, None], axis=1, dtype=jnp.int32)
    place = jnp.concatenate([jnp.stack([y, c, z]).astype(jnp.int32), starts])
    short = short_taps.reshape(short_taps.shape[0], -1)
    bias = skip[None, :]

    every = 2 * length * ctx * xs * tp * width * 3 * width
    raw, rim = call(
        functools.partial(project, ys, offsets),
        (
            jax.ShapeDtypeStruct((length, 3 * width), BF16),
            jax.ShapeDtypeStruct((LEAD, 3 * width), BF16),
        ),
        [SMEM] + [HBM] * (2 * ys + 1),
        (VMEM, VMEM),
        [
            pltpu.VMEM((length, 3 * width), F32),
            pltpu.VMEM((ys, xs, tp, length, width), BF16),
            pltpu.VMEM(weights.shape, BF16),
            pltpu.SemaphoreType.DMA((3 * ctx,)),
        ],
        flops=every,
        nbytes=16 * MIB,
        vmem=VMEM_DOT,
    )(place, *blocks, *others, weights)
    before = lax.ppermute(rim, "ctx", [(k, k + 1) for k in range(ctx - 1)])
    work = lambda rows, wide_rows: [
        pltpu.VMEM((wide_rows, 3 * width), F32),
        pltpu.VMEM((rows, width), F32),
        pltpu.VMEM((length, width), F32),
        pltpu.VMEM((reach + GROUP, width), F32),
        pltpu.VMEM((LEAD + length, width), jnp.int32),
    ]
    outline = jax.ShapeDtypeStruct((length, width), BF16)
    top = jax.ShapeDtypeStruct((HEAD - PAD, width), F32)
    part, *tops = call(
        main_part,
        (outline, top, top),
        [SMEM] + [VMEM] * 4,
        (VMEM, VMEM, VMEM),
        work(length, length),
        flops=every // 2,
        nbytes=2 * MIB,
    )(place, raw, short, mr_taps, bias)
    gated = call(
        head_part,
        outline,
        [SMEM] + [VMEM] * 8,
        VMEM,
        work(LEAD + HEAD, LEAD + PAD),
        flops=every // 4,
        nbytes=1 * MIB,
    )(place, before, raw, short, mr_taps, bias, part, *tops)
    return gated[None]


def solution(mesh):
    in_specs = (
        P(None, "ctx", ("fsdp", "tp")),
        P("ctx", None, ("fsdp", "tp")),
        P(None, None, ("fsdp", "tp")),
        P(None, ("fsdp", "tp")),
        P(("fsdp", "tp")),
        P(),
    )
    out_specs = P(None, "ctx", ("fsdp", "tp"))
    return jax.shard_map(body, mesh=mesh, in_specs=in_specs, out_specs=out_specs, check_vma=False)
```

```python
import functools

import jax
import jax.numpy as jnp
from jax import lax
from jax.experimental import pallas as pl
from jax.experimental.pallas import tpu as pltpu
from jax.sharding import PartitionSpec as P

PAD = 16
LEAD = 128 + PAD
HEAD = 192
STEP = 128
AHEAD = 8
VMEM_DOT = 52
GROUP = 64
BF16, F32 = jnp.bfloat16, jnp.float32
VMEM = pl.BlockSpec(memory_space=pltpu.VMEM)
SMEM = pl.BlockSpec(memory_space=pltpu.SMEM)
ANY = pl.BlockSpec(memory_space=pl.ANY)
HBM = pl.BlockSpec(memory_space=pltpu.HBM)
MIB = 1 << 20


def call(kernel, out_shape, in_specs, out_specs, scratch=(), flops=0, nbytes=0, vmem=8):
    return pl.pallas_call(
        kernel,
        out_shape=out_shape,
        in_specs=in_specs,
        out_specs=out_specs,
        scratch_shapes=list(scratch),
        compiler_params=pltpu.CompilerParams(vmem_limit_bytes=vmem * MIB),
        cost_estimate=pl.CostEstimate(flops=flops, bytes_accessed=nbytes, transcendentals=0),
    )


def wide(planes, groups=None):
    return jnp.concatenate([planes[j] for j in range(planes.shape[0])], 1)


def project(count, offsets, place, *refs):
    mine, other = refs[:count], refs[count : 2 * count]
    weights_in, raw, rim, total, held, weights, sem = refs[2 * count :]
    core = place[1]

    def copies(k):
        slot = lax.rem(place[0] + offsets[k] + count, count)
        return [
            pltpu.make_async_copy(mine[k], held.at[k, :, core], sem.at[3 * k]),
            pltpu.make_async_copy(other[k], held.at[k, :, 1 - core], sem.at[3 * k + 1]),
            pltpu.make_async_copy(weights_in.at[slot], weights.at[k], sem.at[3 * k + 2]),
        ]

    for k in range(min(AHEAD, count)):
        for copy in copies(k):
            copy.start()
    for k in range(count):
        if k + AHEAD < count:
            for copy in copies(k + AHEAD):
                copy.start()
        for copy in copies(k):
            copy.wait()
        left = [held[k, j, c] for j in range(held.shape[1]) for c in range(held.shape[2])]
        term = jnp.dot(jnp.concatenate(left, 1), wide(weights[k]), preferred_element_type=F32)
        if k == 0:
            total[...] = term
        elif k < count - 1:
            total[...] += term
        else:
            rounded = (total[...] + term).astype(BF16)
            raw[...] = rounded
            rim[...] = rounded[rounded.shape[0] - rim.shape[0] :]


def genome(place, row):
    total = (row >= place[3]).astype(jnp.int32)
    for g in (4, 5):
        total = total + (row >= place[g]).astype(jnp.int32)
    return jnp.where(row < 0, -1, total)


def fill(place, length, ids):
    row = lax.broadcasted_iota(jnp.int32, ids.shape, 0) + (place[2] * length - LEAD)
    ids[...] = genome(place, row)


def features(first, last, shift, raw, ids, taps, mixed, queries):
    reach = taps.shape[0] - 1
    for base in range(first, last, STEP):
        step = min(STEP, last - base)
        near = ids[base + LEAD - PAD : base + LEAD + step, :]
        begin = base + shift - PAD
        sums = [jnp.zeros((step, 128), F32) for _ in range(3)]
        for g in range(3):
            if g == 0 and base < 0:
                continue
            held = raw[begin : begin + PAD + step, 128 * g : 128 * g + 128]
            for lag in range(reach + 1):
                spot = slice(PAD - lag, PAD - lag + step)
                weight = taps[lag : lag + 1, 128 * g : 128 * g + 128]
                same = near[spot] == near[PAD:]
                sums[g] = sums[g] + jnp.where(same, held[spot] * weight, 0.0)
        if base >= 0:
            queries[base : base + step, :] = sums[0]
        mixed[base + shift : base + shift + step, :] = (sums[1] * sums[2]).astype(BF16).astype(F32)


def long_filter(first, last, shift, place, ids, mixed, queries, taps, skip, out, window):
    reach = taps.shape[0]

    def group(i, _):
        base = pl.multiple_of(first + i * GROUP, GROUP)
        here = ids[pl.ds(base + LEAD, GROUP), :]

        def one(g, total):
            for k in range((reach + GROUP) // GROUP):
                spot = pl.ds(base + k * GROUP + LEAD - reach, GROUP)
                source = pl.ds(pl.multiple_of(base + k * GROUP + shift - reach, PAD), GROUP)
                window[k * GROUP : k * GROUP + GROUP, :] = jnp.where(
                    ids[spot, :] == g, mixed[source, :], 0.0
                )
            sums = jnp.zeros((GROUP, 128), F32)
            for s in range(8):
                held = window[8 - s : GROUP + reach - s, :]
                for a in range(reach // 8):
                    weight = taps[8 * a + s : 8 * a + s + 1, :]
                    start = reach - 8 - 8 * a
                    sums = sums + held[start : start + GROUP] * weight
            return jnp.where(here == g, sums, total)

        row = place[2] * out.shape[0] + base
        low, high = genome(place, row), genome(place, row + GROUP - 1)
        total = lax.fori_loop(low, high + 1, one, jnp.zeros((GROUP, 128), F32))
        bias = skip[...] * mixed[pl.ds(pl.multiple_of(base + shift, PAD), GROUP), :]
        gated = queries[pl.ds(base, GROUP), :] * (total + bias)
        out[pl.ds(base, GROUP), :] = gated.astype(out.dtype)
        return 0

    lax.fori_loop(0, (last - first) // GROUP, group, 0)


def main_part(
    place, raw, short, taps, skip, out, top_mixed, top_queries, wider, mixed, queries, window, ids
):
    rows = raw.shape[0]
    fill(place, rows, ids)
    wider[...] = raw[...].astype(F32)
    features(PAD, rows, 0, wider, ids, short, mixed, queries)
    top_mixed[...] = mixed[PAD:HEAD, :]
    top_queries[...] = queries[PAD:HEAD, :]
    long_filter(HEAD, rows, 0, place, ids, mixed, queries, taps, skip, out, window)


def head_part(
    place, before, raw, short, taps, skip, given, top_mixed, top_queries,
    out, wider, mixed, queries, window, ids,
):
    rim = before.shape[0]
    fill(place, out.shape[0], ids)
    wider[:rim, :] = before[...].astype(F32)
    wider[rim:, :] = raw[:PAD, :].astype(F32)
    features(PAD - rim, 0, rim, wider, ids, short, mixed, queries)
    features(0, PAD, rim, wider, ids, short, mixed, queries)
    mixed[rim + PAD :, :] = top_mixed[...]
    queries[PAD:HEAD, :] = top_queries[...]
    out[HEAD:, :] = given[HEAD:, :]
    long_filter(0, HEAD, rim, place, ids, mixed, queries, taps, skip, out, window)


def two_way(block, axis, count, hop):
    blocks, offsets, up, down = [block], [0], block, block
    for s in range(1, count // 2 + 1):
        up = lax.ppermute(up, axis, hop(1))
        blocks.append(up)
        offsets.append(-s)
        if s <= (count - 1) // 2:
            down = lax.ppermute(down, axis, hop(-1))
            blocks.append(down)
            offsets.append(s)
    return blocks, tuple(offsets)


def body(tokens, w_in, short_taps, mr_taps, skip, genome_ids):
    length, width = tokens.shape[1], tokens.shape[2]
    ctx, tp = lax.axis_size("ctx"), lax.axis_size("tp")
    xs, ys = lax.axis_size("fsdp") // ctx, ctx
    reach = mr_taps.shape[0]
    f, z, c = lax.axis_index("fsdp"), lax.axis_index("ctx"), lax.axis_index("tp")
    x, y = f % xs, f // xs

    along_x = lambda d: [(j * xs + i, j * xs + (i + d) % xs) for j in range(ys) for i in range(xs)]
    along_y = lambda d: [(j * xs + i, (j + d) % ys * xs + i) for j in range(ys) for i in range(xs)]
    swap = [(0, 1), (1, 0)]

    weights = lax.all_gather(jnp.transpose(w_in, (1, 0, 2)), "ctx", axis=0)

    own = tokens[0]
    block = jnp.zeros((xs,) + own.shape, BF16)
    block = lax.dynamic_update_index_in_dim(block, own, x, 0)
    for d in range(1, xs):
        hop = d if d <= xs // 2 else d - xs
        piece = lax.ppermute(own, "fsdp", along_x(hop))
        block = lax.dynamic_update_index_in_dim(block, piece, (x - hop) % xs, 0)
    blocks, offsets = two_way(block, "fsdp", ys, along_y)
    others = [lax.ppermute(b, "tp", swap) for b in blocks]

    starts = jnp.sum(genome_ids[0][None, :] < jnp.arange(1, 4)[:, None], axis=1, dtype=jnp.int32)
    place = jnp.concatenate([jnp.stack([y, c, z]).astype(jnp.int32), starts])
    short = short_taps.reshape(short_taps.shape[0], -1)
    bias = skip[None, :]

    every = 2 * length * ctx * xs * tp * width * 3 * width
    raw, rim = call(
        functools.partial(project, ys, offsets),
        (
            jax.ShapeDtypeStruct((length, 3 * width), BF16),
            jax.ShapeDtypeStruct((LEAD, 3 * width), BF16),
        ),
        [SMEM] + [HBM] * (2 * ys + 1),
        (VMEM, VMEM),
        [
            pltpu.VMEM((length, 3 * width), F32),
            pltpu.VMEM((ys, xs, tp, length, width), BF16),
            pltpu.VMEM(weights.shape, BF16),
            pltpu.SemaphoreType.DMA((3 * ctx,)),
        ],
        flops=every,
        nbytes=16 * MIB,
        vmem=VMEM_DOT,
    )(place, *blocks, *others, weights)
    before = lax.ppermute(rim, "ctx", [(k, k + 1) for k in range(ctx - 1)])
    work = lambda rows, wide_rows: [
        pltpu.VMEM((wide_rows, 3 * width), F32),
        pltpu.VMEM((rows, width), F32),
        pltpu.VMEM((length, width), F32),
        pltpu.VMEM((reach + GROUP, width), F32),
        pltpu.VMEM((LEAD + length, width), jnp.int32),
    ]
    outline = jax.ShapeDtypeStruct((length, width), BF16)
    top = jax.ShapeDtypeStruct((HEAD - PAD, width), F32)
    part, *tops = call(
        main_part,
        (outline, top, top),
        [SMEM] + [VMEM] * 4,
        (VMEM, VMEM, VMEM),
        work(length, length),
        flops=every // 2,
        nbytes=2 * MIB,
    )(place, raw, short, mr_taps, bias)
    gated = call(
        head_part,
        outline,
        [SMEM] + [VMEM] * 8,
        VMEM,
        work(LEAD + HEAD, LEAD + PAD),
        flops=every // 4,
        nbytes=1 * MIB,
    )(place, before, raw, short, mr_taps, bias, part, *tops)
    return gated[None]


def solution(mesh):
    in_specs = (
        P(None, "ctx", ("fsdp", "tp")),
        P("ctx", None, ("fsdp", "tp")),
        P(None, None, ("fsdp", "tp")),
        P(None, ("fsdp", "tp")),
        P(("fsdp", "tp")),
        P(),
    )
    out_specs = P(None, "ctx", ("fsdp", "tp"))
    return jax.shard_map(body, mesh=mesh, in_specs=in_specs, out_specs=out_specs, check_vma=False)
```
